512 devices in a mesh: enc: 8 (over x, core), llm: 4 (over y), sp: 16 (over z).
Axes of the slice: x: 4, y: 4, z: 16, core: 2. Of those that a mesh axis runs over, the one named last changes fastest.
Arguments:
- text_qkv: bfloat16 [8, 4, 2048, 5120], P('enc', 'llm', 'sp'), may hold values from -12 to 12
- segments: int32 [8, 4, 2048], P('enc', 'llm', 'sp'), may hold values from 0 to 31, never falling along the last dimension, each value on 1 to 256 neighbouring positions
- image_qkv: bfloat16 [8, 4, 16, 64, 5120], P('enc', 'llm', 'sp'), may hold values from -6 to 6
- patch_counts: int32 [8, 4, 16, 2], P('enc', 'llm', 'sp'), may hold values from 8 to 32, as said below
- image_dest: int32 [8, 4, 16, 64], P('enc', 'llm', 'sp'), may hold values from 0 to 31, as said below
- image_offset: int32 [8, 4, 16, 64], P('enc', 'llm', 'sp'), may hold values from 0 to 127, as said below
- output_cotangent: bfloat16 [8, 4, 2048, 4096], P('enc', 'llm', 'sp'), may hold values from -6 to 6
Outputs:
- text_grad: bfloat16 [8, 4, 2048, 5120], P('enc', 'llm', 'sp')
- image_grad: bfloat16 [8, 4, 16, 64, 5120], P('enc', 'llm', 'sp')
The draws below stay inside these ranges and needn't reach their ends.
Inputs may be any that keep to these rules, and one draw needn't show every extreme that they name: `patch_counts`: each encoder shard has 2 images, one of exactly 32 patches; rows past an image's count are padding and their entries are not used. `image_dest`: from each encoder shard at most 4 live rows go to any one slab, and exactly 4 go to one slab that is drawn separately for each shard, so it may differ from shard to shard. `image_offset`: live rows that go to the same slab and sp index never share a position.
All inputs are finite; a program needn't handle non-finite values.
Results may differ from the reference program's by a relative error of at most 0.014.
Values may be sent and summed in bfloat16 or wider, within the bound.
A program may use at most 64 MiB of HBM per device.

```python
import math
import jax
import jax.numpy as jnp
import numpy as np
from jax import lax

QUERY_HEADS = 32
KEY_VALUE_HEADS = 4
HEAD_SIZE = 128
TOK_DEV = 128
SEG_MAX = 256
PATCH_MAX = 32
IMGS_DEV = 2
IMG_DEV = 64
SLAB = 2048
C = 5120
N_ENC = 8
N_LLM = 4
N_SP = 16


def route_plan(key):
    query_groups = N_ENC * N_LLM
    capacity = TOK_DEV // query_groups
    slot_total = query_groups * capacity
    key_number, key_big, key_first, key_slot, key_place = jax.random.split(key, 5)
    leading_dims = (N_ENC, N_LLM, N_SP)
    counts = jax.random.randint(key_number, leading_dims + (IMGS_DEV,), PATCH_MAX // 4, PATCH_MAX + 1)
    biggest = jax.random.randint(key_big, leading_dims, 0, IMGS_DEV)
    counts = jnp.where(jnp.arange(IMGS_DEV)[None, None, None, :] == biggest[..., None], PATCH_MAX, counts).astype(jnp.int32)
    chosen = jax.random.randint(key_first, leading_dims, 0, query_groups)
    slot_ids = jnp.arange(slot_total, dtype=jnp.int32)
    scores = jax.random.randint(key_slot, leading_dims + (slot_total,), 0, 1 << 20) * slot_total + slot_ids
    forced = (slot_ids // capacity)[None, None, None, :] == chosen[..., None]
    scores = jnp.where(forced, slot_ids % capacity - slot_total, scores)
    ordered = jnp.argsort(scores, axis=-1)
    row_ids = jnp.arange(IMG_DEV, dtype=jnp.int32)
    patch_ids = row_ids % PATCH_MAX
    image_ids = row_ids // PATCH_MAX
    row_keys = jnp.where((image_ids[None, None, None, :] == biggest[..., None]) & (patch_ids < capacity)[None, None, None, :], patch_ids[None, None, None, :], capacity + row_ids[None, None, None, :])
    ranks = jnp.argsort(jnp.argsort(row_keys, axis=-1), axis=-1)
    slot_of = jnp.take_along_axis(ordered, ranks, axis=-1)
    destination = (slot_of // capacity).astype(jnp.int32)
    within = slot_of % capacity
    place_scores = jax.random.randint(key_place, (query_groups, N_SP, TOK_DEV), 0, 1 << 20) * TOK_DEV + jnp.arange(TOK_DEV, dtype=jnp.int32)
    placement = jnp.argsort(place_scores, axis=-1).astype(jnp.int32)
    source = jnp.arange(N_ENC, dtype=jnp.int32)[:, None] * N_LLM + jnp.arange(N_LLM, dtype=jnp.int32)[None, :]
    index_in = source[:, :, None, None] * capacity + within
    sp_ids = jnp.arange(N_SP, dtype=jnp.int32)[None, None, :, None]
    offsets = placement[destination, sp_ids, index_in].astype(jnp.int32)
    return (counts, destination, offsets)


def draw_patch_counts(key, part):
    plan = route_plan(key)
    return plan[0]


def draw_image_dest(key, part):
    plan = route_plan(key)
    return plan[1]


def draw_image_offset(key, part):
    plan = route_plan(key)
    return plan[2]


def draw_text_qkv(key, part):
    key = jax.random.fold_in(key, 4)
    leading_dims = (N_ENC, N_LLM, SLAB)
    every_head = QUERY_HEADS + 2 * KEY_VALUE_HEADS
    whole = jnp.clip(jax.random.normal(key, leading_dims + (every_head, HEAD_SIZE)), -6.0, 6.0)
    return whole.reshape(leading_dims + (every_head * HEAD_SIZE,)).astype(jnp.bfloat16)


def levels(rng, extent, cuts, low, largest):
    def one(dim, shards_of):
        heights = jax.random.uniform(jax.random.fold_in(jax.random.fold_in(rng, 6), dim), (shards_of,), jnp.float32, low / len(cuts), largest / len(cuts))
        return jnp.repeat(jnp.exp(heights), extent[dim] // shards_of).reshape((-1,) + (1,) * (len(extent) - dim - 1))

    loudness = one(*cuts[0])
    for cut in cuts[1:]:
        loudness = loudness * one(*cut)
    return loudness


def profile(number_of, total, most, skew):
    portions = [(1 << 20) // math.isqrt(standing ** skew) + 1 for standing in range(2, number_of + 1)]
    rest, given = total - most - (number_of - 1), [1] * (number_of - 1)
    while rest > 0:
        free = [i for i in range(number_of - 1) if given[i] < most]
        whole, budget = sum([portions[i] for i in free]), rest
        for i in free:
            extra = min(most - given[i], max(1, budget * portions[i] // whole), rest)
            given[i] = given[i] + extra
            rest = rest - extra
    return np.array([most] + given)


def ragged(own_key, count, total, limit, slope):
    if count == 2:
        one = jax.random.randint(own_key, (), max(1, total - limit), min(limit, total - 1) + 1)
        return jnp.stack([one, total - one])
    tallies = jnp.asarray(profile(count, total, limit, slope), jnp.int32)
    twos = (count - 1) // 2
    donor, taker = tallies[1:1 + 2 * twos:2], tallies[2:2 + 2 * twos:2]
    room = jnp.minimum(donor - 1, limit - taker)
    moved = jax.random.randint(jax.random.fold_in(own_key, 1), (twos,), 0, 1 << 20) % (room + 1)
    tallies = tallies.at[1:1 + 2 * twos:2].set(donor - moved).at[2:2 + 2 * twos:2].set(taker + moved)
    return tallies[jax.random.permutation(jax.random.fold_in(own_key, 2), count)]


def bell_draw(own_key, extent, deviation, limit, pieces=(), kind=jnp.bfloat16):
    level = levels(own_key, extent, pieces, -0.22, 0.18) if pieces else 1.0
    drawn = jax.random.normal(own_key, extent, jnp.float32) * deviation * level
    return jnp.minimum(jnp.maximum(drawn, -limit), limit).astype(kind)


def setup_inputs(seed: int = 0) -> dict:
    streams_of = jax.random.split(jax.random.key(seed), 8)
    return {
        "text_qkv": draw_text_qkv(jax.random.fold_in(streams_of[7], 71), 0),
        "segments": jax.vmap(lambda own: jnp.searchsorted(jnp.cumsum(ragged(own, SLAB * 4 // SEG_MAX, SLAB, SEG_MAX, 0)), jnp.arange(SLAB), side="right"))(jax.random.split(streams_of[1], N_ENC * N_LLM)).reshape((N_ENC, N_LLM, SLAB)).astype(jnp.int32),
        "image_qkv": bell_draw(streams_of[2], (N_ENC, N_LLM, N_SP, IMG_DEV, C), 1.0, 6.0, ((0, 8), (1, 4), (2, 16))),
        "patch_counts": draw_patch_counts(jax.random.fold_in(streams_of[7], 71), 0),
        "image_dest": draw_image_dest(jax.random.fold_in(streams_of[7], 71), 0),
        "image_offset": draw_image_offset(jax.random.fold_in(streams_of[7], 71), 0),
        "output_cotangent": bell_draw(streams_of[6], (N_ENC, N_LLM, SLAB, QUERY_HEADS * HEAD_SIZE), 1.0, 6.0, ((0, 8), (1, 4), (2, 16))),
    }


NEG_FILL = -1e30


def block_grads(query_rows, every_key, query_seg, key_seg, query_pos, key_pos, row_gradient):
    query_groups = QUERY_HEADS // KEY_VALUE_HEADS
    scale = HEAD_SIZE ** -0.5
    total_rows = query_rows.shape[0]
    total_keys = every_key.shape[0]
    queries_four = query_rows.astype(jnp.float32).reshape(total_rows, KEY_VALUE_HEADS, query_groups, HEAD_SIZE)
    keys_four = every_key[:, :KEY_VALUE_HEADS * HEAD_SIZE].astype(jnp.float32).reshape(total_keys, KEY_VALUE_HEADS, HEAD_SIZE)
    values_four = every_key[:, KEY_VALUE_HEADS * HEAD_SIZE:].astype(jnp.float32).reshape(total_keys, KEY_VALUE_HEADS, HEAD_SIZE)
    gradient_four = row_gradient.astype(jnp.float32).reshape(total_rows, KEY_VALUE_HEADS, query_groups, HEAD_SIZE)
    visible = (query_seg[:, None] == key_seg[None, :]) & (key_pos[None, :] <= query_pos[:, None]) & (key_pos[None, :] >= 0)
    logits = jnp.einsum("qhgd,khd->hgqk", queries_four, keys_four) * scale
    logits = jnp.where(visible[None, None], logits, NEG_FILL)
    top = jnp.max(logits, axis=-1, keepdims=True)
    log_total = top + jnp.log(jnp.sum(jnp.exp(logits - top), axis=-1, keepdims=True))
    probs = jnp.exp(logits - log_total)
    probs_b = lax.optimization_barrier(probs.astype(jnp.bfloat16)).astype(jnp.float32)
    attended = jnp.einsum("hgqk,khd->qhgd", probs_b, values_four)
    attended = lax.optimization_barrier(attended.astype(jnp.bfloat16)).astype(jnp.float32)
    delta = jnp.transpose(jnp.sum(gradient_four * attended, axis=-1), (1, 2, 0))[..., None]
    value_gradient = jnp.einsum("hgqk,qhgd->khd", probs_b, gradient_four)
    grad_probs = jnp.einsum("qhgd,khd->hgqk", gradient_four, values_four)
    grad_logits = probs * (grad_probs - delta) * scale
    grad_logits = lax.optimization_barrier(grad_logits.astype(jnp.bfloat16)).astype(jnp.float32)
    grad_queries = jnp.einsum("hgqk,khd->qhgd", grad_logits, keys_four)
    key_gradient = jnp.einsum("hgqk,qhgd->khd", grad_logits, queries_four)
    key_value_gradient = jnp.concatenate([key_gradient.reshape(total_keys, KEY_VALUE_HEADS * HEAD_SIZE), value_gradient.reshape(total_keys, KEY_VALUE_HEADS * HEAD_SIZE)], axis=1)
    return grad_queries.reshape(total_rows, QUERY_HEADS * HEAD_SIZE).astype(jnp.bfloat16), key_value_gradient


def slab_grads(slab_pair):
    slab_rows, slab_seg, slab_grad_out = slab_pair
    halo_depth = (SEG_MAX + TOK_DEV - 2) // TOK_DEV
    back = halo_depth * TOK_DEV
    q_width = QUERY_HEADS * HEAD_SIZE
    key_value_width = 2 * KEY_VALUE_HEADS * HEAD_SIZE
    padded_kv = jnp.concatenate([jnp.zeros((back, key_value_width), slab_rows.dtype), slab_rows[:, q_width:]], axis=0)
    padded_seg = jnp.concatenate([jnp.zeros((back,), jnp.int32), slab_seg.astype(jnp.int32)], axis=0)
    padded_pos = jnp.arange(SLAB + back, dtype=jnp.int32) - back
    all_queries = slab_rows[:, :q_width]

    def one_block(block_index):
        first_row = (block_index * TOK_DEV).astype(jnp.int32)
        query_rows = lax.dynamic_slice_in_dim(all_queries, first_row, TOK_DEV, 0)
        query_seg = lax.dynamic_slice_in_dim(slab_seg.astype(jnp.int32), first_row, TOK_DEV, 0)
        query_pos = first_row + jnp.arange(TOK_DEV, dtype=jnp.int32)
        row_gradient = lax.dynamic_slice_in_dim(slab_grad_out, first_row, TOK_DEV, 0)
        every_key = lax.dynamic_slice_in_dim(padded_kv, first_row, back + TOK_DEV, 0)
        key_seg = lax.dynamic_slice_in_dim(padded_seg, first_row, back + TOK_DEV, 0)
        key_pos = lax.dynamic_slice_in_dim(padded_pos, first_row, back + TOK_DEV, 0)
        return block_grads(query_rows, every_key, query_seg, key_seg, query_pos, key_pos, row_gradient)

    def add_block(running, pair_item):
        block_index, piece = pair_item
        first_row = (block_index * TOK_DEV).astype(jnp.int32)
        current = lax.dynamic_slice_in_dim(running, first_row, back + TOK_DEV, 0)
        return lax.dynamic_update_slice_in_dim(running, current + piece, first_row, 0), None

    block_ids = jnp.arange(SLAB // TOK_DEV, dtype=jnp.int32)
    grad_q, key_value_gradient = lax.map(one_block, block_ids)
    running, unused = lax.scan(add_block, jnp.zeros((SLAB + back, key_value_width), jnp.float32), (block_ids, key_value_gradient))
    return jnp.concatenate([grad_q.reshape(SLAB, q_width), running[back:].astype(jnp.bfloat16)], axis=1)


def reference(text_qkv, segments, image_qkv, patch_counts, image_dest, image_offset, output_cotangent):
    width_per_row = (QUERY_HEADS + 2 * KEY_VALUE_HEADS) * HEAD_SIZE
    slab_total = N_ENC * N_LLM
    row_ids = jnp.arange(IMGS_DEV * PATCH_MAX, dtype=jnp.int32)
    row_count = patch_counts[..., row_ids // PATCH_MAX]
    is_live = (row_ids % PATCH_MAX) < row_count
    sp_ids = jnp.arange(N_SP, dtype=jnp.int32)[None, None, :, None]
    target = image_dest * SLAB + sp_ids * TOK_DEV + image_offset
    target = jnp.where(is_live, target, slab_total * SLAB).astype(jnp.int32).reshape(-1)
    flat_text = text_qkv.reshape(slab_total * SLAB, width_per_row)
    slab_rows = flat_text.at[target].set(image_qkv.reshape(-1, width_per_row), mode="drop")
    is_image = jnp.zeros((slab_total * SLAB,), jnp.int32).at[target].set(1, mode="drop")
    grads = lax.map(slab_grads, (slab_rows.reshape(slab_total, SLAB, width_per_row), segments.reshape(slab_total, SLAB), output_cotangent.reshape(slab_total, SLAB, QUERY_HEADS * HEAD_SIZE)))
    grads = grads.reshape(slab_total * SLAB, width_per_row)
    text_grad = jnp.where(is_image[:, None] > 0, jnp.zeros_like(grads), grads).reshape(text_qkv.shape)
    picked = grads[jnp.minimum(target, slab_total * SLAB - 1)]
    image_grad = jnp.where(is_live.reshape(-1)[:, None], picked, jnp.zeros_like(picked)).reshape(image_qkv.shape)
    return text_grad, image_grad
```

```python
import jax
import jax.numpy as jnp
from jax import lax
from jax.experimental import pallas as pl
from jax.experimental.pallas import tpu as pltpu
from jax.sharding import PartitionSpec as P

QUERY_HEADS = 32
KEY_VALUE_HEADS = 4
HEAD_SIZE = 128
TOK = 128
IMG = 64
PATCHES = 32
N_ENC = 8
N_LLM = 4
N_SP = 16
PEERS = N_ENC * N_LLM
SLOTS = 4
COLS = (QUERY_HEADS + 2 * KEY_VALUE_HEADS) * HEAD_SIZE
GROUP = QUERY_HEADS // KEY_VALUE_HEADS
KEYS = 3 * TOK
KV = 4
PART = 1024
SCALE = HEAD_SIZE ** (-0.5)
EXP2_SCALE = SCALE * 1.4426950408889634
HIDDEN = -1e30

MESH = pl.DeviceIdType.MESH
F32 = jnp.float32
BF16 = jnp.bfloat16
I32 = jnp.int32


def iota(shape, dim):
    return lax.broadcasted_iota(I32, shape, dim)


def dot(a, b):
    return jnp.dot(a, b, preferred_element_type=F32)


def dot_t(a, b):
    return lax.dot_general(a, b, (((1,), (1,)), ((), ())), preferred_element_type=F32)


def as_column(row, size):
    eye = iota((size, size), 0) == iota((size, size), 1)
    return jnp.sum(jnp.where(eye, row, 0.0), axis=1, keepdims=True)


def one_hot(condition):
    return jnp.where(condition, 1.0, 0.0).astype(BF16)


def kernel(
    text_hbm, seg_hbm, img_hbm, count_hbm, dest_hbm, offset_hbm, cot_hbm,
    text_out, image_out,
    text, seg, img, count, dest, offset, cot,
    mark_out, mark_in, row_out, row_in, grad_out, grad_in, seg_in,
    pack, unpack, place, collect, bias, image_mask,
    kv, queries, probs_t, ds_t, far, near, own, far_in, pass_out, pass_in, kv_grad,
    text_grad, image_grad,
    load_sem, store_sem, mark_send, mark_recv, row_send, row_recv, grad_send, grad_recv,
    seg_send, seg_recv, kv_send, kv_recv, relay_send, relay_recv,
    far_send, far_recv, pass_send, pass_recv,
):
    e, l, s = lax.axis_index("enc"), lax.axis_index("llm"), lax.axis_index("sp")
    me = e * N_LLM + l
    up, up2, down, down2 = (lax.rem(s + d, N_SP) for d in (1, 2, N_SP - 1, N_SP - 2))

    loads = [
        pltpu.make_async_copy(src, dst, load_sem.at[i])
        for i, (src, dst) in enumerate(
            (
                (dest_hbm, dest), (offset_hbm, offset), (count_hbm, count), (seg_hbm, seg),
                (img_hbm, img), (text_hbm, text), (cot_hbm, cot),
            )
        )
    ]
    for load in loads:
        load.start()

    barrier = pltpu.get_barrier_semaphore()

    def peer(i):
        p = lax.rem(me + i, PEERS)
        return p, (p // N_LLM, lax.rem(p, N_LLM), s)

    def greet(i, carry):
        pl.semaphore_signal(barrier, inc=1, device_id=peer(i)[1], device_id_type=MESH)
        return carry

    lax.fori_loop(1, PEERS, greet, 0)
    for z in (down, down2, up):
        pl.semaphore_signal(barrier, inc=1, device_id=(e, l, z), device_id_type=MESH)

    for load in loads[:3]:
        load.wait()
    row_id = iota((1, IMG), 1)
    counts = jnp.where(row_id < PATCHES, count[:, 0:1], count[:, 1:2])
    live_row = lax.rem(row_id, PATCHES) < counts
    dest_row = jnp.where(live_row, dest[...], -1).astype(F32)
    dest_col = as_column(dest_row, IMG)
    offset_col = as_column(offset[...].astype(F32), IMG)
    same = (dest_col == dest_row) & (dest_row >= 0.0)
    lower = iota((IMG, IMG), 1) < iota((IMG, IMG), 0)
    higher = iota((IMG, IMG), 0) < iota((IMG, IMG), 1)
    rank_col = jnp.sum(jnp.where(same & lower, 1.0, 0.0), axis=1, keepdims=True)
    rank_row = jnp.sum(jnp.where(same & higher, 1.0, 0.0), axis=0, keepdims=True)
    slot_row = jnp.where(dest_row >= 0.0, dest_row * SLOTS + rank_row, -1.0)
    slot_col = jnp.where(dest_col >= 0.0, dest_col * SLOTS + rank_col, -1.0)
    repeat = one_hot(lax.rem(iota((IMG, 4 * IMG), 1), IMG) == iota((IMG, 4 * IMG), 0))
    slots_row = dot(jnp.broadcast_to(slot_row, (8, IMG)).astype(BF16), repeat)[0:1, :]
    tall = iota((16 * PEERS, 4 * IMG), 0)
    wide = iota((16 * PEERS, 4 * IMG), 1)
    pack[...] = one_hot(
        ((tall // 16 * SLOTS + lax.rem(tall, 4)).astype(F32) == slots_row)
        & (lax.rem(tall // 4, 4) == wide // IMG)
    )
    to_whom = one_hot(iota((PEERS, IMG), 0).astype(F32) == dest_row)
    lane = iota((IMG, TOK), 1)
    marks_mine = jnp.where(
        lane.astype(F32) == (me * SLOTS).astype(F32) + rank_col, offset_col + 1.0, 0.0
    ).astype(BF16)
    marks = dot(to_whom, marks_mine).astype(I32)
    for d in range(PEERS):
        mark_out[d] = marks[d : d + 1, :]
    mark_in[pl.ds(me, 1)] = mark_out[pl.ds(me, 1)]

    def four_tall(read):
        return jnp.concatenate(
            [jnp.concatenate([read(t, b) for b in range(4)], axis=0) for t in range(2)], axis=1
        )

    def columns(part, t, b):
        return pl.ds(pl.multiple_of(part * PART + t * 512 + b * 128, 128), 128)

    def pack_rows(part):
        packed = dot(pack[...], four_tall(lambda t, b: img[:, columns(part, t, b)])).astype(BF16)
        for t in range(2):
            row_out[part, :, t] = packed[:, t * 128 : (t + 1) * 128].reshape(PEERS, 16, 128)
        row_in[part, pl.ds(me, 1)] = row_out[part, pl.ds(me, 1)]

    def row_copy(part, i):
        p, device = peer(i)
        return pltpu.make_async_remote_copy(
            src_ref=row_out.at[part, p], dst_ref=row_in.at[part, me],
            send_sem=row_send.at[part], recv_sem=row_recv.at[part],
            device_id=device, device_id_type=MESH,
        )

    def grad_copy(part, i):
        p, device = peer(i)
        return pltpu.make_async_remote_copy(
            src_ref=grad_out.at[part, p], dst_ref=grad_in.at[part, me],
            send_sem=grad_send.at[part], recv_sem=grad_recv.at[part],
            device_id=device, device_id_type=MESH,
        )

    def mark_copy(i):
        p, device = peer(i)
        return pltpu.make_async_remote_copy(
            src_ref=mark_out.at[p], dst_ref=mark_in.at[me],
            send_sem=mark_send, recv_sem=mark_recv,
            device_id=device, device_id_type=MESH,
        )

    def start_all(copy_of):
        def one(i, carry):
            copy_of(i).start()
            return carry

        lax.fori_loop(1, PEERS, one, 0)

    def all_rows(part):
        return pltpu.make_async_remote_copy(
            src_ref=row_out.at[part, 0 : PEERS - 1], dst_ref=row_in.at[part, 0 : PEERS - 1],
            send_sem=row_send.at[part], recv_sem=row_recv.at[part],
            device_id=(e, l, up), device_id_type=MESH,
        )

    def all_grads(part):
        return pltpu.make_async_remote_copy(
            src_ref=grad_out.at[part, 0 : PEERS - 1], dst_ref=grad_in.at[part, 0 : PEERS - 1],
            send_sem=grad_send.at[part], recv_sem=grad_recv.at[part],
            device_id=(e, l, up), device_id_type=MESH,
        )

    all_marks = pltpu.make_async_remote_copy(
        src_ref=mark_out.at[0 : PEERS - 1], dst_ref=mark_in.at[0 : PEERS - 1],
        send_sem=mark_send, recv_sem=mark_recv, device_id=(e, l, up), device_id_type=MESH,
    )

    loads[4].wait()
    pack_rows(KV)
    loads[3].wait()
    pl.semaphore_wait(barrier, PEERS + 2)
    start_all(mark_copy)
    start_all(lambda i: row_copy(KV, i))
    seg_copies = [
        pltpu.make_async_remote_copy(
            src_ref=seg, dst_ref=seg_in.at[i], send_sem=seg_send.at[i], recv_sem=seg_recv.at[i],
            device_id=(e, l, z), device_id_type=MESH,
        )
        for i, z in enumerate((up, up2))
    ]
    for copy in seg_copies:
        copy.start()

    def send_queries(part, carry):
        pack_rows(part)
        start_all(lambda i: row_copy(part, i))
        return carry

    lax.fori_loop(0, KEY_VALUE_HEADS, send_queries, 0)

    slots_col = jnp.concatenate([slot_col] * 4, axis=0)
    tall = iota((4 * IMG, 16 * PEERS), 0)
    wide = iota((4 * IMG, 16 * PEERS), 1)
    unpack[...] = one_hot(
        ((wide // 16 * SLOTS + lax.rem(wide, 4)).astype(F32) == slots_col)
        & (lax.rem(wide // 4, 4) == tall // IMG)
    )

    all_marks.wait_recv()
    marks_row = jnp.sum(mark_in[...], axis=0).astype(F32)
    spread = one_hot(
        iota((TOK, 16 * PEERS), 0)
        == iota((TOK, 16 * PEERS), 1) // 16 * SLOTS + lax.rem(iota((TOK, 16 * PEERS), 1), 4)
    )
    spread_row = dot(jnp.broadcast_to(marks_row, (8, TOK)).astype(BF16), spread)[0:1, :]
    tall = iota((4 * TOK, 16 * PEERS), 0)
    wide = iota((4 * TOK, 16 * PEERS), 1)
    place[...] = one_hot(
        ((lax.rem(tall, TOK) + 1).astype(F32) == spread_row)
        & (tall // TOK == lax.rem(wide // 4, 4))
    )
    tall = iota((16 * PEERS, TOK), 0)
    wide = iota((16 * PEERS, TOK), 1)
    spread_col = jnp.sum(
        jnp.where(wide == tall // 16 * SLOTS + lax.rem(tall, 4), marks_row, 0.0),
        axis=1, keepdims=True,
    )
    tall = iota((16 * PEERS, 4 * TOK), 0)
    wide = iota((16 * PEERS, 4 * TOK), 1)
    collect[...] = one_hot(
        ((lax.rem(wide, TOK) + 1).astype(F32) == spread_col)
        & (wide // TOK == lax.rem(tall // 4, 4))
    )
    taken = jnp.sum(
        jnp.where((iota((TOK, TOK), 0) + 1).astype(F32) == marks_row, 1.0, 0.0),
        axis=1, keepdims=True,
    )
    image_mask[...] = jnp.broadcast_to(taken, (TOK, TOK))

    loads[5].wait()

    def placed(part):
        arrived = jnp.concatenate(
            [row_in[part, :, t].reshape(16 * PEERS, 128) for t in range(2)], axis=1
        )
        landed = dot(place[...], arrived)

        def block(t, b):
            rows = landed[b * 128 : (b + 1) * 128, t * 128 : (t + 1) * 128]
            text_rows = text[:, columns(part, t, b)].astype(F32)
            return jnp.where(image_mask[...] > 0.0, rows, text_rows).astype(BF16)

        return block

    def masked(rows):
        return jnp.where(image_mask[...] > 0.0, 0.0, rows).astype(BF16)

    def next_copy(g):
        return pltpu.make_async_remote_copy(
            src_ref=kv.at[g, 2 * TOK : 3 * TOK], dst_ref=kv.at[g, TOK : 2 * TOK],
            send_sem=kv_send.at[g], recv_sem=kv_recv.at[g],
            device_id=(e, l, up), device_id_type=MESH,
        )

    def relay_copy(g):
        return pltpu.make_async_remote_copy(
            src_ref=kv.at[g, TOK : 2 * TOK], dst_ref=kv.at[g, 0:TOK],
            send_sem=relay_send.at[g], recv_sem=relay_recv.at[g],
            device_id=(e, l, up), device_id_type=MESH,
        )

    def far_copy(g):
        return pltpu.make_async_remote_copy(
            src_ref=far.at[g], dst_ref=far_in.at[g],
            send_sem=far_send.at[g], recv_sem=far_recv.at[g],
            device_id=(e, l, down), device_id_type=MESH,
        )

    def pass_copy(g):
        return pltpu.make_async_remote_copy(
            src_ref=pass_out.at[g], dst_ref=pass_in.at[g],
            send_sem=pass_send.at[g], recv_sem=pass_recv.at[g],
            device_id=(e, l, down), device_id_type=MESH,
        )

    all_rows(KV).wait_recv()
    block = placed(KV)
    for g in range(KEY_VALUE_HEADS):
        for t in range(2):
            kv[g, 2 * TOK : 3 * TOK, t * 128 : (t + 1) * 128] = block(t, g)
        next_copy(g).start()

    for copy in seg_copies:
        copy.wait_recv()
    seg_row = seg[...].astype(F32)
    seg_near = jnp.where(s >= 1, as_column(seg_in[0].astype(F32), TOK), -1.0)
    seg_far = jnp.where(s >= 2, as_column(seg_in[1].astype(F32), TOK), -1.0)
    seg_own = as_column(seg_row, TOK)
    for i, column in enumerate((seg_far, seg_near, seg_own)):
        visible = column == seg_row
        if i == 2:
            visible = visible & (iota((TOK, TOK), 0) <= iota((TOK, TOK), 1))
        hidden = jnp.where(visible, 0.0, HIDDEN)
        for h in range(2):
            bias[i * TOK : (i + 1) * TOK, h * 128 : (h + 1) * 128] = hidden

    def relay(g):
        next_copy(g).wait_recv()
        relay_copy(g).start()

    def chain(g):
        far_copy(g).wait_recv()
        pass_out[g] = (near[g] + far_in[g].astype(F32)).astype(BF16)
        pass_copy(g).start()

    def finish(g):
        pass_copy(g).wait_recv()
        total = (own[g] + pass_in[g].astype(F32)).astype(BF16)
        kv_grad[g] = total
        for t in range(2):
            text_grad[:, columns(KV, t, g)] = masked(
                total[:, t * 128 : (t + 1) * 128].astype(F32)
            )

    def return_rows(part, read):
        gathered = dot(collect[...], four_tall(read)).astype(BF16)
        for t in range(2):
            grad_out[part, :, t] = gathered[:, t * 128 : (t + 1) * 128].reshape(PEERS, 16, 128)
        grad_in[part, pl.ds(me, 1)] = grad_out[part, pl.ds(me, 1)]
        start_all(lambda i: grad_copy(part, i))

    def part_columns(part):
        return pl.ds(pl.multiple_of(part * PART, PART), PART)

    def text_store(part):
        return pltpu.make_async_copy(
            text_grad.at[:, part_columns(part)], text_out.at[:, part_columns(part)],
            store_sem.at[0, part],
        )

    def image_store(part):
        return pltpu.make_async_copy(
            image_grad.at[:, part_columns(part)], image_out.at[:, part_columns(part)],
            store_sem.at[1, part],
        )

    eye = one_hot(iota((128, 128), 0) == iota((128, 128), 1))
    loads[6].wait()
    relay(0)
    relay(1)

    def group(g, carry):
        all_rows(g).wait_recv()
        block = placed(g)
        for t in range(2):
            for b in range(4):
                h = t * 4 + b
                queries[h * 128 : (h + 1) * 128, :] = block(t, b)

        @pl.when(g < 2)
        def _():
            relay(g + 2)

        relay_copy(g).wait_recv()
        keys = kv[g, :, 0:128]
        values = kv[g, :, 128:256]
        keys_t = dot_t(eye, keys).astype(BF16)
        cots = [
            cot[:, pl.ds(pl.multiple_of(g * PART + h * 128, 128), 128)] for h in range(GROUP)
        ]
        grads = []
        for pair in range(GROUP // 2):
            q = queries[pair * 256 : (pair + 1) * 256, :]
            d_out = jnp.concatenate(cots[2 * pair : 2 * pair + 2], axis=0)
            logits = dot_t(keys, q) + bias[...]
            top = jnp.max(logits, axis=0, keepdims=True)
            raised = jnp.exp2((logits - top) * EXP2_SCALE)
            inverse = 1.0 / jnp.sum(raised, axis=0, keepdims=True)
            grad_probs = dot_t(values, d_out)
            delta = jnp.sum(raised * grad_probs, axis=0, keepdims=True) * inverse
            probs_t[:, pair * 256 : (pair + 1) * 256] = (raised * inverse).astype(BF16)
            ds = (raised * ((grad_probs - delta) * (inverse * SCALE))).astype(BF16)
            ds_t[:, pair * 256 : (pair + 1) * 256] = ds
            grad_t = dot(keys_t, ds).astype(BF16)
            for i in range(2):
                grads.append(dot_t(eye, grad_t[:, i * 128 : (i + 1) * 128]).astype(BF16))
        key_grad = dot(ds_t[...], queries[...])
        value_grad = dot(probs_t[...], jnp.concatenate(cots, axis=0))
        for t, grad in enumerate((key_grad, value_grad)):
            half = slice(t * 128, (t + 1) * 128)
            far[g, :, half] = grad[0:TOK].astype(BF16)
            near[g, :, half] = grad[TOK : 2 * TOK]
            own[g, :, half] = grad[2 * TOK : 3 * TOK]
        far_copy(g).start()
        return_rows(g, lambda t, b: grads[t * 4 + b])
        for t in range(2):
            for b in range(4):
                text_grad[:, columns(g, t, b)] = masked(grads[t * 4 + b].astype(F32))
        text_store(g).start()

        @pl.when(g >= 1)
        def _():
            chain(g - 1)

        @pl.when(g >= 2)
        def _():
            finish(g - 2)

        return carry

    lax.fori_loop(0, KEY_VALUE_HEADS, group, 0)
    chain(3)
    finish(2)
    finish(3)
    return_rows(KV, lambda t, b: kv_grad[b, :, t * 128 : (t + 1) * 128])
    text_store(KV).start()

    def take_back(part, carry):
        all_grads(part).wait_recv()
        returned = jnp.concatenate(
            [grad_in[part, :, t].reshape(16 * PEERS, 128) for t in range(2)], axis=1
        )
        back = dot(unpack[...], returned).astype(BF16)
        for t in range(2):
            for b in range(4):
                image_grad[:, columns(part, t, b)] = back[
                    b * IMG : (b + 1) * IMG, t * 128 : (t + 1) * 128
                ]
        image_store(part).start()
        return carry

    lax.fori_loop(0, KV + 1, take_back, 0)

    all_marks.wait_send()
    for copy in seg_copies:
        copy.wait_send()

    def drain(part, carry):
        all_rows(part).wait_send()
        all_grads(part).wait_send()
        text_store(part).wait()
        image_store(part).wait()
        return carry

    lax.fori_loop(0, KV + 1, drain, 0)

    def drain_halo(g, carry):
        for copy in (next_copy, relay_copy, far_copy, pass_copy):
            copy(g).wait_send()
        return carry

    lax.fori_loop(0, KEY_VALUE_HEADS, drain_halo, 0)


def body(text_qkv, segments, image_qkv, patch_counts, image_dest, image_offset, output_cotangent):
    hbm = pl.BlockSpec(memory_space=pl.ANY)
    dma = pltpu.SemaphoreType.DMA
    q_cols = QUERY_HEADS * HEAD_SIZE
    tiles = (KV + 1, PEERS, 2, 16, 128)
    halo = (KEY_VALUE_HEADS, TOK, 256)
    text_grad, image_grad = pl.pallas_call(
        kernel,
        name="slab",
        out_shape=(
            jax.ShapeDtypeStruct((TOK, COLS), BF16),
            jax.ShapeDtypeStruct((IMG, COLS), BF16),
        ),
        in_specs=[hbm] * 7,
        out_specs=(hbm, hbm),
        scratch_shapes=[
            pltpu.VMEM((TOK, COLS), BF16),
            pltpu.VMEM((1, TOK), I32),
            pltpu.VMEM((IMG, COLS), BF16),
            pltpu.VMEM((1, 2), I32),
            pltpu.VMEM((1, IMG), I32),
            pltpu.VMEM((1, IMG), I32),
            pltpu.VMEM((TOK, q_cols), BF16),
            pltpu.VMEM((PEERS, 1, TOK), I32),
            pltpu.VMEM((PEERS, 1, TOK), I32),
            pltpu.VMEM(tiles, BF16),
            pltpu.VMEM(tiles, BF16),
            pltpu.VMEM(tiles, BF16),
            pltpu.VMEM(tiles, BF16),
            pltpu.VMEM((2, 1, TOK), I32),
            pltpu.VMEM((16 * PEERS, 4 * IMG), BF16),
            pltpu.VMEM((4 * IMG, 16 * PEERS), BF16),
            pltpu.VMEM((4 * TOK, 16 * PEERS), BF16),
            pltpu.VMEM((16 * PEERS, 4 * TOK), BF16),
            pltpu.VMEM((KEYS, 256), F32),
            pltpu.VMEM((TOK, 128), F32),
            pltpu.VMEM((KEY_VALUE_HEADS, KEYS, 256), BF16),
            pltpu.VMEM((GROUP * TOK, 128), BF16),
            pltpu.VMEM((KEYS, GROUP * TOK), BF16),
            pltpu.VMEM((KEYS, GROUP * TOK), BF16),
            pltpu.VMEM(halo, BF16),
            pltpu.VMEM(halo, F32),
            pltpu.VMEM(halo, F32),
            pltpu.VMEM(halo, BF16),
            pltpu.VMEM(halo, BF16),
            pltpu.VMEM(halo, BF16),
            pltpu.VMEM(halo, BF16),
            pltpu.VMEM((TOK, COLS), BF16),
            pltpu.VMEM((IMG, COLS), BF16),
            dma((7,)),
            dma((2, KV + 1)),
            dma, dma,
            dma((KV + 1,)), dma((KV + 1,)), dma((KV + 1,)), dma((KV + 1,)),
            dma((2,)), dma((2,)),
            dma((4,)), dma((4,)), dma((4,)), dma((4,)),
            dma((4,)), dma((4,)), dma((4,)), dma((4,)),
        ],
        compiler_params=pltpu.CompilerParams(
            collective_id=0, has_side_effects=True, vmem_limit_bytes=56 << 20
        ),
        cost_estimate=pl.CostEstimate(
            flops=4 << 30, bytes_accessed=5 << 20, transcendentals=2 << 20
        ),
    )(
        text_qkv[0, 0], segments[0], image_qkv[0, 0, 0], patch_counts[0, 0],
        image_dest[0, 0], image_offset[0, 0], output_cotangent[0, 0],
    )
    return text_grad[None, None], image_grad[None, None, None]


def solution(mesh):
    rows = P("enc", "llm", "sp", None)
    deep = P("enc", "llm", "sp", None, None)
    return jax.shard_map(
        body, mesh=mesh,
        in_specs=(rows, P("enc", "llm", "sp"), deep, rows, rows, rows, rows),
        out_specs=(rows, deep), check_vma=False,
    )
```

```python
import jax
import jax.numpy as jnp
from jax import lax
from jax.experimental import pallas as pl
from jax.experimental.pallas import tpu as pltpu
from jax.sharding import PartitionSpec as P

QUERY_HEADS = 32
KEY_VALUE_HEADS = 4
HEAD_SIZE = 128
TOK = 128
IMG = 64
PATCHES = 32
N_ENC = 8
N_LLM = 4
N_SP = 16
PEERS = N_ENC * N_LLM
SLOTS = 4
COLS = (QUERY_HEADS + 2 * KEY_VALUE_HEADS) * HEAD_SIZE
GROUP = QUERY_HEADS // KEY_VALUE_HEADS
KEYS = 3 * TOK
PARTS = 6
PART = 1024
SCALE = HEAD_SIZE ** (-0.5)
EXP2_SCALE = SCALE * 1.4426950408889634
HIDDEN = -1e30

MESH = pl.DeviceIdType.MESH
F32 = jnp.float32
BF16 = jnp.bfloat16
I32 = jnp.int32


def iota(shape, dim):
    return lax.broadcasted_iota(I32, shape, dim)


def dot(a, b):
    return jnp.dot(a, b, preferred_element_type=F32)


def dot_t(a, b):
    return lax.dot_general(a, b, (((1,), (1,)), ((), ())), preferred_element_type=F32)


def as_column(row, size):
    eye = iota((size, size), 0) == iota((size, size), 1)
    return jnp.sum(jnp.where(eye, row, 0.0), axis=1, keepdims=True)


def one_hot(condition):
    return jnp.where(condition, 1.0, 0.0).astype(BF16)


def kernel(
    text_hbm, seg_hbm, img_hbm, count_hbm, dest_hbm, offset_hbm, cot_hbm,
    text_grad, image_grad,
    text, seg, img, count, dest, offset, cot,
    mark_out, mark_in, row_out, row_in, grad_out, grad_in,
    kv_rows_out, kv_rows_in, kv_grads_out, kv_grads_in, seg_in,
    pack, unpack, place, collect, bias, causal, image_mask,
    kv, queries, probs_t, ds_t, far, near, own, far_in, pass_out, pass_in, kv_grad,
    load_sem, mark_send, mark_recv, row_send, row_recv, grad_send, grad_recv,
    seg_send, seg_recv, kv_send, kv_recv, relay_send, relay_recv,
    far_send, far_recv, pass_send, pass_recv,
):
    e, l, s = lax.axis_index("enc"), lax.axis_index("llm"), lax.axis_index("sp")
    me = e * N_LLM + l
    up, up2, down, down2 = (lax.rem(s + d, N_SP) for d in (1, 2, N_SP - 1, N_SP - 2))

    loads = [
        pltpu.make_async_copy(src, dst, load_sem.at[i])
        for i, (src, dst) in enumerate(
            (
                (dest_hbm, dest), (offset_hbm, offset), (count_hbm, count), (seg_hbm, seg),
                (img_hbm, img), (text_hbm, text), (cot_hbm, cot),
            )
        )
    ]
    for load in loads:
        load.start()

    barrier = pltpu.get_barrier_semaphore()

    def peer(i):
        p = lax.rem(me + i, PEERS)
        return p, (p // N_LLM, lax.rem(p, N_LLM), s)

    def greet(i, carry):
        pl.semaphore_signal(barrier, inc=1, device_id=peer(i)[1], device_id_type=MESH)
        return carry

    lax.fori_loop(1, PEERS, greet, 0)
    for z in (down, down2, up):
        pl.semaphore_signal(barrier, inc=1, device_id=(e, l, z), device_id_type=MESH)

    for load in loads[:3]:
        load.wait()
    row_id = iota((1, IMG), 1)
    counts = jnp.where(row_id < PATCHES, count[:, 0:1], count[:, 1:2])
    live_row = lax.rem(row_id, PATCHES) < counts
    dest_row = jnp.where(live_row, dest[...], -1).astype(F32)
    dest_col = as_column(dest_row, IMG)
    offset_col = as_column(offset[...].astype(F32), IMG)
    same = (dest_col == dest_row) & (dest_row >= 0.0)
    lower = iota((IMG, IMG), 1) < iota((IMG, IMG), 0)
    higher = iota((IMG, IMG), 0) < iota((IMG, IMG), 1)
    rank_col = jnp.sum(jnp.where(same & lower, 1.0, 0.0), axis=1, keepdims=True)
    rank_row = jnp.sum(jnp.where(same & higher, 1.0, 0.0), axis=0, keepdims=True)
    slot_row = jnp.where(dest_row >= 0.0, dest_row * SLOTS + rank_row, -1.0)
    slot_col = jnp.where(dest_col >= 0.0, dest_col * SLOTS + rank_col, -1.0)
    repeat = one_hot(lax.rem(iota((IMG, 4 * IMG), 1), IMG) == iota((IMG, 4 * IMG), 0))
    slots_row = dot(jnp.broadcast_to(slot_row, (8, IMG)).astype(BF16), repeat)[0:1, :]
    codes_row = slots_row.astype(I32) * 4 + iota((1, 4 * IMG), 1) // IMG
    pack[...] = one_hot(iota((16 * PEERS, 4 * IMG), 0) == codes_row)
    to_whom = one_hot(iota((PEERS, IMG), 0).astype(F32) == dest_row)
    lane = iota((IMG, TOK), 1)
    marks_mine = jnp.where(
        lane.astype(F32) == (me * SLOTS).astype(F32) + rank_col, offset_col + 1.0, 0.0
    ).astype(BF16)
    marks = dot(to_whom, marks_mine).astype(I32)
    for d in range(PEERS):
        mark_out[d] = marks[d : d + 1, :]
    mark_in[pl.ds(me, 1)] = mark_out[pl.ds(me, 1)]

    def four_tall(read, tiles):
        return jnp.concatenate(
            [jnp.concatenate([read(t, b) for b in range(4)], axis=0) for t in tiles], axis=1
        )

    def q_columns(g, t, b):
        return pl.ds(pl.multiple_of(g * PART + t * 512 + b * 128, 128), 128)

    def kv_columns(g, t):
        return slice(4096 + t * 512 + g * 128, 4096 + t * 512 + g * 128 + 128)

    def pack_queries(g):
        packed = dot(pack[...], four_tall(lambda t, b: img[:, q_columns(g, t, b)], (0, 1)))
        packed = packed.astype(BF16)
        for t in range(2):
            row_out[g, :, t] = packed[:, t * 128 : (t + 1) * 128].reshape(PEERS, 16, 128)
        row_in[g, pl.ds(me, 1)] = row_out[g, pl.ds(me, 1)]

    def pack_kv():
        packed = dot(
            pack[...],
            four_tall(lambda t, b: img[:, kv_columns(2 * t + b // 2, b % 2)], (0, 1)),
        ).astype(BF16)
        for t in range(2):
            kv_rows_out[t] = packed[:, t * 128 : (t + 1) * 128].reshape(PEERS, 16, 128)
            kv_rows_in[t, pl.ds(me, 1)] = kv_rows_out[t, pl.ds(me, 1)]

    def scatter(source, target, send_sem, recv_sem):
        def copy_of(i):
            p, device = peer(i)
            return pltpu.make_async_remote_copy(
                src_ref=source.at[p], dst_ref=target.at[me], send_sem=send_sem,
                recv_sem=recv_sem, device_id=device, device_id_type=MESH,
            )

        def three(n, carry):
            for i in range(3):
                copy_of(n * 3 + i + 1).start()
            return carry

        lax.fori_loop(0, (PEERS - 1) // 3, three, 0)
        copy_of(PEERS - 1).start()

    def whole(source, target, send_sem, recv_sem):
        return pltpu.make_async_remote_copy(
            src_ref=source.at[0 : PEERS - 1], dst_ref=target.at[0 : PEERS - 1],
            send_sem=send_sem, recv_sem=recv_sem, device_id=(e, l, up), device_id_type=MESH,
        )

    def rows_of(g):
        return row_out.at[g], row_in.at[g], row_send.at[g], row_recv.at[g]

    def kv_rows_of(t):
        return kv_rows_out.at[t], kv_rows_in.at[t], row_send.at[4 + t], row_recv.at[4 + t]

    def grads_of(g):
        return grad_out.at[g], grad_in.at[g], grad_send.at[g], grad_recv.at[g]

    def kv_grads_of(t):
        return kv_grads_out.at[t], kv_grads_in.at[t], grad_send.at[4 + t], grad_recv.at[4 + t]

    marks_of = (mark_out, mark_in, mark_send, mark_recv)

    loads[4].wait()
    pack_kv()
    loads[3].wait()
    pl.semaphore_wait(barrier, PEERS + 2)
    scatter(*marks_of)
    scatter(*kv_rows_of(0))
    scatter(*kv_rows_of(1))
    seg_copies = [
        pltpu.make_async_remote_copy(
            src_ref=seg, dst_ref=seg_in.at[i], send_sem=seg_send.at[i], recv_sem=seg_recv.at[i],
            device_id=(e, l, z), device_id_type=MESH,
        )
        for i, z in enumerate((up, up2))
    ]
    for copy in seg_copies:
        copy.start()

    def send_queries(g, carry):
        pack_queries(g)
        scatter(*rows_of(g))
        return carry

    lax.fori_loop(0, KEY_VALUE_HEADS, send_queries, 0)

    slots_col = jnp.concatenate([slot_col] * 4, axis=0)
    codes_col = slots_col.astype(I32) * 4 + iota((4 * IMG, 1), 0) // IMG
    unpack[...] = one_hot(codes_col == iota((4 * IMG, 16 * PEERS), 1))

    for copy in seg_copies:
        copy.wait_recv()
    seg_row = seg[...].astype(F32)
    seg_near = jnp.where(s >= 1, as_column(seg_in[0].astype(F32), TOK), -1.0)
    seg_far = jnp.where(s >= 2, as_column(seg_in[1].astype(F32), TOK), -1.0)
    seg_own = as_column(seg_row, TOK)
    earlier = iota((TOK, TOK), 0) <= iota((TOK, TOK), 1)
    near_bias = jnp.where(seg_near == seg_row, 0.0, HIDDEN)
    rest_bias = jnp.where(jnp.where(earlier, seg_own, seg_far) == seg_row, 0.0, HIDDEN)
    for h in range(2):
        half = slice(h * 128, (h + 1) * 128)
        bias[0:TOK, half] = rest_bias
        bias[TOK : 2 * TOK, half] = near_bias
        causal[:, half] = jnp.where(earlier, 1.0, 0.0)

    whole(*marks_of).wait_recv()
    marks_row = jnp.sum(mark_in[...], axis=0).astype(F32)
    spread = one_hot(iota((TOK, 16 * PEERS), 0) == iota((TOK, 16 * PEERS), 1) // 4)
    spread_row = dot(jnp.broadcast_to(marks_row, (8, TOK)).astype(BF16), spread)[0:1, :]
    codes_row = spread_row.astype(I32) + lax.rem(iota((1, 16 * PEERS), 1), 4) * 256
    tall = iota((4 * TOK, 1), 0)
    codes_col = lax.rem(tall, TOK) + 1 + tall // TOK * 256
    place[...] = one_hot(codes_col == codes_row)
    taken = jnp.sum(
        jnp.where((iota((TOK, TOK), 0) + 1).astype(F32) == marks_row, 1.0, 0.0),
        axis=1, keepdims=True,
    )
    image_mask[...] = jnp.broadcast_to(taken, (TOK, TOK))
    loads[5].wait()

    def mixed(landed, text_rows):
        return jnp.where(image_mask[...] > 0.0, landed, text_rows.astype(F32)).astype(BF16)

    def masked(rows):
        return jnp.where(image_mask[...] > 0.0, 0.0, rows).astype(BF16)

    def next_copy(g):
        return pltpu.make_async_remote_copy(
            src_ref=kv.at[g, 2 * TOK : 3 * TOK], dst_ref=kv.at[g, TOK : 2 * TOK],
            send_sem=kv_send.at[g], recv_sem=kv_recv.at[g],
            device_id=(e, l, up), device_id_type=MESH,
        )

    def relay_copy(g):
        return pltpu.make_async_remote_copy(
            src_ref=kv.at[g, TOK : 2 * TOK], dst_ref=kv.at[g, 0:TOK],
            send_sem=relay_send.at[g], recv_sem=relay_recv.at[g],
            device_id=(e, l, up), device_id_type=MESH,
        )

    def far_copy(g):
        return pltpu.make_async_remote_copy(
            src_ref=far.at[g], dst_ref=far_in.at[g],
            send_sem=far_send.at[g], recv_sem=far_recv.at[g],
            device_id=(e, l, down), device_id_type=MESH,
        )

    def pass_copy(g):
        return pltpu.make_async_remote_copy(
            src_ref=pass_out.at[g], dst_ref=pass_in.at[g],
            send_sem=pass_send.at[g], recv_sem=pass_recv.at[g],
            device_id=(e, l, down), device_id_type=MESH,
        )

    def relay(g):
        next_copy(g).wait_recv()
        relay_copy(g).start()

    def place_kv(t):
        whole(*kv_rows_of(t)).wait_recv()
        landed = dot(place[...], kv_rows_in[t].reshape(16 * PEERS, 128))
        for b in range(4):
            g, half = 2 * t + b // 2, b % 2
            kv[g, 2 * TOK : 3 * TOK, half * 128 : (half + 1) * 128] = mixed(
                landed[b * 128 : (b + 1) * 128], text[:, kv_columns(g, half)]
            )

    place_kv(0)
    next_copy(0).start()
    next_copy(1).start()
    place_kv(1)

    tall = iota((16 * PEERS, TOK), 0)
    spread_col = jnp.sum(
        jnp.where(iota((16 * PEERS, TOK), 1) == tall // 4, marks_row, 0.0),
        axis=1, keepdims=True,
    )
    codes_col = spread_col.astype(I32) + lax.rem(iota((16 * PEERS, 1), 0), 4) * 256
    wide = iota((1, 4 * TOK), 1)
    collect[...] = one_hot(codes_col == lax.rem(wide, TOK) + 1 + wide // TOK * 256)

    relay(0)
    next_copy(2).start()
    relay(1)
    next_copy(3).start()

    def chain(g):
        far_copy(g).wait_recv()
        pass_out[g] = (near[g] + far_in[g].astype(F32)).astype(BF16)
        pass_copy(g).start()

    def finish(g):
        pass_copy(g).wait_recv()
        kv_grad[g] = (own[g] + pass_in[g].astype(F32)).astype(BF16)

    loads[6].wait()

    def group(g, carry):
        whole(*rows_of(g)).wait_recv()
        arrived = jnp.concatenate(
            [row_in[g, :, t].reshape(16 * PEERS, 128) for t in range(2)], axis=1
        )
        landed = dot(place[...], arrived)
        for t in range(2):
            for b in range(4):
                h = t * 4 + b
                queries[h * 128 : (h + 1) * 128, :] = mixed(
                    landed[b * 128 : (b + 1) * 128, t * 128 : (t + 1) * 128],
                    text[:, q_columns(g, t, b)],
                )

        relay_copy(g).wait_recv()
        keys = kv[g, :, 0:128]
        values = kv[g, :, 128:256]
        cots = [
            cot[:, pl.ds(pl.multiple_of(g * PART + h * 128, 128), 128)] for h in range(GROUP)
        ]
        is_own = causal[...] > 0.0
        own_part = causal[...].astype(BF16)
        far_part = (1.0 - causal[...]).astype(BF16)

        def two_blocks(products):
            rest = jnp.where(is_own, products[2 * TOK :], products[0:TOK])
            return jnp.concatenate([rest, products[TOK : 2 * TOK]], axis=0)

        for pair in range(GROUP // 2):
            both = slice(pair * 256, (pair + 1) * 256)
            d_out = jnp.concatenate(cots[2 * pair : 2 * pair + 2], axis=0)
            logits = two_blocks(dot_t(keys, queries[both, :])) + bias[...]
            grad_probs = two_blocks(dot_t(values, d_out))
            top = jnp.max(logits, axis=0, keepdims=True)
            raised = jnp.exp2((logits - top) * EXP2_SCALE)
            inverse = 1.0 / jnp.sum(raised, axis=0, keepdims=True)
            delta = jnp.sum(raised * grad_probs, axis=0, keepdims=True) * inverse
            probs = (raised * inverse).astype(BF16)
            ds = (raised * ((grad_probs - delta) * (inverse * SCALE))).astype(BF16)
            for target, value in ((probs_t, probs), (ds_t, ds)):
                target[0:TOK, both] = value[0:TOK] * far_part
                target[TOK : 2 * TOK, both] = value[TOK : 2 * TOK]
                target[2 * TOK : 3 * TOK, both] = value[0:TOK] * own_part
        key_grad = dot(ds_t[...], queries[...])
        value_grad = dot(probs_t[...], jnp.concatenate(cots, axis=0))
        for t, grad in enumerate((key_grad, value_grad)):
            half = slice(t * 128, (t + 1) * 128)
            far[g, :, half] = grad[0:TOK].astype(BF16)
            near[g, :, half] = grad[TOK : 2 * TOK]
            own[g, :, half] = grad[2 * TOK : 3 * TOK]
        far_copy(g).start()

        @pl.when(g < 2)
        def _():
            relay(g + 2)

        grads_t = dot(keys.T, ds_t[...]).astype(BF16)
        grads = [grads_t[:, h * 128 : (h + 1) * 128].T for h in range(GROUP)]
        gathered = dot(collect[...], four_tall(lambda t, b: grads[t * 4 + b], (0, 1)))
        gathered = gathered.astype(BF16)
        for t in range(2):
            grad_out[g, :, t] = gathered[:, t * 128 : (t + 1) * 128].reshape(PEERS, 16, 128)
        grad_in[g, pl.ds(me, 1)] = grad_out[g, pl.ds(me, 1)]
        scatter(*grads_of(g))

        @pl.when(g >= 1)
        def _():
            chain(g - 1)

        for t in range(2):
            for b in range(4):
                text_grad[:, q_columns(g, t, b)] = masked(grads[t * 4 + b].astype(F32))

        @pl.when(g >= 2)
        def _():
            finish(g - 2)

        return carry

    lax.fori_loop(0, KEY_VALUE_HEADS, group, 0)

    def return_kv(t):
        rows = four_tall(
            lambda _, b: kv_grad[2 * t + b // 2, :, b % 2 * 128 : (b % 2 + 1) * 128], (0,)
        )
        kv_grads_out[t] = dot(collect[...], rows).astype(BF16).reshape(PEERS, 16, 128)
        kv_grads_in[t, pl.ds(me, 1)] = kv_grads_out[t, pl.ds(me, 1)]
        scatter(*kv_grads_of(t))

    def take_back(g, carry):
        whole(*grads_of(g)).wait_recv()
        returned = jnp.concatenate(
            [grad_in[g, :, t].reshape(16 * PEERS, 128) for t in range(2)], axis=1
        )
        back = dot(unpack[...], returned).astype(BF16)
        for t in range(2):
            for b in range(4):
                image_grad[:, q_columns(g, t, b)] = back[
                    b * IMG : (b + 1) * IMG, t * 128 : (t + 1) * 128
                ]
        return carry

    return_kv(0)
    chain(3)
    finish(2)
    take_back(0, 0)
    finish(3)
    return_kv(1)
    for g in range(KEY_VALUE_HEADS):
        for t in range(2):
            text_grad[:, kv_columns(g, t)] = masked(
                kv_grad[g, :, t * 128 : (t + 1) * 128].astype(F32)
            )
    lax.fori_loop(1, KEY_VALUE_HEADS, take_back, 0)

    whole(*marks_of).wait_send()
    for copy in seg_copies:
        copy.wait_send()

    def drain(g, carry):
        whole(*rows_of(g)).wait_send()
        whole(*grads_of(g)).wait_send()
        for copy in (next_copy, relay_copy, far_copy, pass_copy):
            copy(g).wait_send()
        return carry

    lax.fori_loop(0, KEY_VALUE_HEADS, drain, 0)
    for t in range(2):
        whole(*kv_rows_of(t)).wait_send()
        whole(*kv_grads_of(t)).wait()
        back = dot(unpack[...], kv_grads_in[t].reshape(16 * PEERS, 128)).astype(BF16)
        for b in range(4):
            image_grad[:, kv_columns(2 * t + b // 2, b % 2)] = back[b * IMG : (b + 1) * IMG]


def write_out(text_grad, image_grad, text_out, image_out, sem):
    copies = [
        pltpu.make_async_copy(text_grad, text_out, sem.at[0]),
        pltpu.make_async_copy(image_grad, image_out, sem.at[1]),
    ]
    for copy in copies:
        copy.start()
    for copy in copies:
        copy.wait()


def body(text_qkv, segments, image_qkv, patch_counts, image_dest, image_offset, output_cotangent):
    hbm = pl.BlockSpec(memory_space=pl.ANY)
    dma = pltpu.SemaphoreType.DMA
    q_cols = QUERY_HEADS * HEAD_SIZE
    tiles = (KEY_VALUE_HEADS, PEERS, 2, 16, 128)
    kv_tiles = (2, PEERS, 16, 128)
    vmem = pl.BlockSpec(memory_space=pltpu.VMEM)
    halo = (KEY_VALUE_HEADS, TOK, 256)
    text_grad, image_grad = pl.pallas_call(
        kernel,
        name="slab",
        out_shape=(pltpu.VMEM((TOK, COLS), BF16), pltpu.VMEM((IMG, COLS), BF16)),
        in_specs=[pl.BlockSpec(memory_space=pltpu.HBM)] * 7,
        out_specs=(vmem, vmem),
        scratch_shapes=[
            pltpu.VMEM((TOK, COLS), BF16),
            pltpu.VMEM((1, TOK), I32),
            pltpu.VMEM((IMG, COLS), BF16),
            pltpu.VMEM((1, 2), I32),
            pltpu.VMEM((1, IMG), I32),
            pltpu.VMEM((1, IMG), I32),
            pltpu.VMEM((TOK, q_cols), BF16),
            pltpu.VMEM((PEERS, 1, TOK), I32),
            pltpu.VMEM((PEERS, 1, TOK), I32),
            pltpu.VMEM(tiles, BF16),
            pltpu.VMEM(tiles, BF16),
            pltpu.VMEM(tiles, BF16),
            pltpu.VMEM(tiles, BF16),
            pltpu.VMEM(kv_tiles, BF16),
            pltpu.VMEM(kv_tiles, BF16),
            pltpu.VMEM(kv_tiles, BF16),
            pltpu.VMEM(kv_tiles, BF16),
            pltpu.VMEM((2, 1, TOK), I32),
            pltpu.VMEM((16 * PEERS, 4 * IMG), BF16),
            pltpu.VMEM((4 * IMG, 16 * PEERS), BF16),
            pltpu.VMEM((4 * TOK, 16 * PEERS), BF16),
            pltpu.VMEM((16 * PEERS, 4 * TOK), BF16),
            pltpu.VMEM((2 * TOK, 256), F32),
            pltpu.VMEM((TOK, 256), F32),
            pltpu.VMEM((TOK, 128), F32),
            pltpu.VMEM((KEY_VALUE_HEADS, KEYS, 256), BF16),
            pltpu.VMEM((GROUP * TOK, 128), BF16),
            pltpu.VMEM((KEYS, GROUP * TOK), BF16),
            pltpu.VMEM((KEYS, GROUP * TOK), BF16),
            pltpu.VMEM(halo, BF16),
            pltpu.VMEM(halo, F32),
            pltpu.VMEM(halo, F32),
            pltpu.VMEM(halo, BF16),
            pltpu.VMEM(halo, BF16),
            pltpu.VMEM(halo, BF16),
            pltpu.VMEM(halo, BF16),
            dma((7,)),
            dma, dma,
            dma((PARTS,)), dma((PARTS,)), dma((PARTS,)), dma((PARTS,)),
            dma((2,)), dma((2,)),
            dma((4,)), dma((4,)), dma((4,)), dma((4,)),
            dma((4,)), dma((4,)), dma((4,)), dma((4,)),
        ],
        compiler_params=pltpu.CompilerParams(
            collective_id=0, has_side_effects=True, vmem_limit_bytes=58 << 20
        ),
        cost_estimate=pl.CostEstimate(
            flops=4 << 30, bytes_accessed=5 << 20, transcendentals=2 << 20
        ),
    )(
        text_qkv[0, 0], segments[0], image_qkv[0, 0, 0], patch_counts[0, 0],
        image_dest[0, 0], image_offset[0, 0], output_cotangent[0, 0],
    )
    text_grad, image_grad = pl.pallas_call(
        write_out,
        name="write_out",
        out_shape=(
            jax.ShapeDtypeStruct((TOK, COLS), BF16),
            jax.ShapeDtypeStruct((IMG, COLS), BF16),
        ),
        in_specs=[vmem, vmem],
        out_specs=(hbm, hbm),
        scratch_shapes=[dma((2,))],
        compiler_params=pltpu.CompilerParams(vmem_limit_bytes=4 << 20),
    )(text_grad, image_grad)
    return text_grad[None, None], image_grad[None, None, None]


def solution(mesh):
    rows = P("enc", "llm", "sp", None)
    deep = P("enc", "llm", "sp", None, None)
    return jax.shard_map(
        body, mesh=mesh,
        in_specs=(rows, P("enc", "llm", "sp"), deep, rows, rows, rows, rows),
        out_specs=(rows, deep), check_vma=False,
    )
```

```python
import jax
import jax.numpy as jnp
from jax import lax
from jax.experimental import pallas as pl
from jax.experimental.pallas import tpu as pltpu
from jax.sharding import PartitionSpec as P

QUERY_HEADS = 32
KEY_VALUE_HEADS = 4
HEAD_SIZE = 128
TOK = 128
IMG = 64
PATCHES = 32
N_ENC = 8
N_LLM = 4
N_SP = 16
PEERS = N_ENC * N_LLM
SLOTS = 4
COLS = (QUERY_HEADS + 2 * KEY_VALUE_HEADS) * HEAD_SIZE
GROUP = QUERY_HEADS // KEY_VALUE_HEADS
KEYS = 3 * TOK
PARTS = 6
PART = 1024
SCALE = HEAD_SIZE ** (-0.5)
EXP2_SCALE = SCALE * 1.4426950408889634
HIDDEN = -1e30

MESH = pl.DeviceIdType.MESH
F32 = jnp.float32
BF16 = jnp.bfloat16
I32 = jnp.int32


def iota(shape, dim):
    return lax.broadcasted_iota(I32, shape, dim)


def dot(a, b):
    return jnp.dot(a, b, preferred_element_type=F32)


def dot_t(a, b):
    return lax.dot_general(a, b, (((1,), (1,)), ((), ())), preferred_element_type=F32)


def as_column(row, size):
    eye = iota((size, size), 0) == iota((size, size), 1)
    return jnp.sum(jnp.where(eye, row, 0.0), axis=1, keepdims=True)


def one_hot(condition):
    return jnp.where(condition, 1.0, 0.0).astype(BF16)


def kernel(
    text_hbm, seg_hbm, img_hbm, count_hbm, dest_hbm, offset_hbm, cot_hbm,
    text_grad, image_grad,
    text, seg, img, count, dest, offset, cot,
    mark_out, mark_in, row_out, row_in, grad_out, grad_in,
    kv_rows_out, kv_rows_in, kv_grads_out, kv_grads_in, seg_in,
    pack, unpack, place, collect, bias, causal, image_mask,
    kv, queries, probs_t, ds_t, far, near, own, far_in, pass_out, pass_in, kv_grad,
    load_sem, mark_send, mark_recv, row_send, row_recv, grad_send, grad_recv,
    seg_send, seg_recv, kv_send, kv_recv, relay_send, relay_recv,
    far_send, far_recv, pass_send, pass_recv,
):
    e, l, s = lax.axis_index("enc"), lax.axis_index("llm"), lax.axis_index("sp")
    me = e * N_LLM + l
    up, up2, down, down2 = (lax.rem(s + d, N_SP) for d in (1, 2, N_SP - 1, N_SP - 2))

    loads = [
        pltpu.make_async_copy(src, dst, load_sem.at[i])
        for i, (src, dst) in enumerate(
            (
                (dest_hbm, dest), (offset_hbm, offset), (count_hbm, count), (seg_hbm, seg),
                (img_hbm, img), (text_hbm, text), (cot_hbm, cot),
            )
        )
    ]
    for load in loads:
        load.start()

    barrier = pltpu.get_barrier_semaphore()

    def peer(i):
        p = lax.rem(me + i, PEERS)
        return p, (p // N_LLM, lax.rem(p, N_LLM), s)

    def for_peers(action):
        def some(n, carry):
            for i in range(10):
                action(n * 10 + i + 1)
            return carry

        lax.fori_loop(0, (PEERS - 2) // 10, some, 0)
        action(PEERS - 1)

    for_peers(
        lambda i: pl.semaphore_signal(
            barrier, inc=1, device_id=peer(i)[1], device_id_type=MESH
        )
    )
    for z in (down, down2, up):
        pl.semaphore_signal(barrier, inc=1, device_id=(e, l, z), device_id_type=MESH)

    for load in loads[:3]:
        load.wait()
    row_id = iota((1, IMG), 1)
    counts = jnp.where(row_id < PATCHES, count[:, 0:1], count[:, 1:2])
    live_row = lax.rem(row_id, PATCHES) < counts
    dest_row = jnp.where(live_row, dest[...], -1).astype(F32)
    dest_col = as_column(dest_row, IMG)
    offset_col = as_column(offset[...].astype(F32), IMG)
    same = (dest_col == dest_row) & (dest_row >= 0.0)
    lower = iota((IMG, IMG), 1) < iota((IMG, IMG), 0)
    higher = iota((IMG, IMG), 0) < iota((IMG, IMG), 1)
    rank_col = jnp.sum(jnp.where(same & lower, 1.0, 0.0), axis=1, keepdims=True)
    rank_row = jnp.sum(jnp.where(same & higher, 1.0, 0.0), axis=0, keepdims=True)
    slot_row = jnp.where(dest_row >= 0.0, dest_row * SLOTS + rank_row, -1.0)
    slot_col = jnp.where(dest_col >= 0.0, dest_col * SLOTS + rank_col, -1.0)
    repeat = one_hot(lax.rem(iota((IMG, 4 * IMG), 1), IMG) == iota((IMG, 4 * IMG), 0))
    slots_row = dot(jnp.broadcast_to(slot_row, (8, IMG)).astype(BF16), repeat)[0:1, :]
    codes_row = slots_row.astype(I32) * 4 + iota((1, 4 * IMG), 1) // IMG
    pack[...] = one_hot(iota((16 * PEERS, 4 * IMG), 0) == codes_row)
    to_whom = one_hot(iota((PEERS, IMG), 0).astype(F32) == dest_row)
    lane = iota((IMG, TOK), 1)
    marks_mine = jnp.where(
        lane.astype(F32) == (me * SLOTS).astype(F32) + rank_col, offset_col + 1.0, 0.0
    ).astype(BF16)
    marks = dot(to_whom, marks_mine).astype(I32)
    for d in range(PEERS):
        mark_out[d] = marks[d : d + 1, :]
    mark_in[pl.ds(me, 1)] = mark_out[pl.ds(me, 1)]

    def four_tall(read, tiles):
        return jnp.concatenate(
            [jnp.concatenate([read(t, b) for b in range(4)], axis=0) for t in tiles], axis=1
        )

    def q_columns(g, t, b):
        return pl.ds(pl.multiple_of(g * PART + t * 512 + b * 128, 128), 128)

    def kv_columns(g, t):
        return slice(4096 + t * 512 + g * 128, 4096 + t * 512 + g * 128 + 128)

    def pack_queries(g):
        packed = dot(pack[...], four_tall(lambda t, b: img[:, q_columns(g, t, b)], (0, 1)))
        packed = packed.astype(BF16)
        for t in range(2):
            row_out[g, :, t] = packed[:, t * 128 : (t + 1) * 128].reshape(PEERS, 16, 128)
        row_in[g, pl.ds(me, 1)] = row_out[g, pl.ds(me, 1)]

    def pack_kv(t):
        packed = dot(
            pack[...],
            four_tall(lambda _, b: img[:, kv_columns(2 * t + b // 2, b % 2)], (0,)),
        )
        kv_rows_out[t] = packed.astype(BF16).reshape(PEERS, 16, 128)
        kv_rows_in[t, pl.ds(me, 1)] = kv_rows_out[t, pl.ds(me, 1)]

    def scatter(source, target, send_sem, recv_sem):
        def copy_of(i):
            p, device = peer(i)
            return pltpu.make_async_remote_copy(
                src_ref=source.at[p], dst_ref=target.at[me], send_sem=send_sem,
                recv_sem=recv_sem, device_id=device, device_id_type=MESH,
            )

        for_peers(lambda i: copy_of(i).start())

    def whole(source, target, send_sem, recv_sem):
        return pltpu.make_async_remote_copy(
            src_ref=source.at[0 : PEERS - 1], dst_ref=target.at[0 : PEERS - 1],
            send_sem=send_sem, recv_sem=recv_sem, device_id=(e, l, up), device_id_type=MESH,
        )

    def rows_of(g):
        return row_out.at[g], row_in.at[g], row_send.at[g], row_recv.at[g]

    def kv_rows_of(t):
        return kv_rows_out.at[t], kv_rows_in.at[t], row_send.at[4 + t], row_recv.at[4 + t]

    def grads_of(g):
        return grad_out.at[g], grad_in.at[g], grad_send.at[g], grad_recv.at[g]

    def kv_grads_of(t):
        return kv_grads_out.at[t], kv_grads_in.at[t], grad_send.at[4 + t], grad_recv.at[4 + t]

    marks_of = (mark_out, mark_in, mark_send, mark_recv)

    loads[4].wait()
    pack_kv(0)
    loads[3].wait()
    pl.semaphore_wait(barrier, PEERS + 2)
    scatter(*marks_of)
    scatter(*kv_rows_of(0))
    pack_kv(1)
    scatter(*kv_rows_of(1))
    seg_copies = [
        pltpu.make_async_remote_copy(
            src_ref=seg, dst_ref=seg_in.at[i], send_sem=seg_send.at[i], recv_sem=seg_recv.at[i],
            device_id=(e, l, z), device_id_type=MESH,
        )
        for i, z in enumerate((up, up2))
    ]
    for copy in seg_copies:
        copy.start()

    def send_queries(g, carry):
        pack_queries(g)
        scatter(*rows_of(g))
        return carry

    lax.fori_loop(0, KEY_VALUE_HEADS, send_queries, 0)

    slots_col = jnp.concatenate([slot_col] * 4, axis=0)
    codes_col = slots_col.astype(I32) * 4 + iota((4 * IMG, 1), 0) // IMG
    unpack[...] = one_hot(codes_col == iota((4 * IMG, 16 * PEERS), 1))

    for copy in seg_copies:
        copy.wait_recv()
    seg_row = seg[...].astype(F32)
    seg_near = jnp.where(s >= 1, as_column(seg_in[0].astype(F32), TOK), -1.0)
    seg_far = jnp.where(s >= 2, as_column(seg_in[1].astype(F32), TOK), -1.0)
    seg_own = as_column(seg_row, TOK)
    earlier = iota((TOK, TOK), 0) <= iota((TOK, TOK), 1)
    near_bias = jnp.where(seg_near == seg_row, 0.0, HIDDEN)
    rest_bias = jnp.where(jnp.where(earlier, seg_own, seg_far) == seg_row, 0.0, HIDDEN)
    for h in range(2):
        half = slice(h * 128, (h + 1) * 128)
        bias[0:TOK, half] = rest_bias
        bias[TOK : 2 * TOK, half] = near_bias
        causal[:, half] = jnp.where(earlier, 1.0, 0.0)

    whole(*marks_of).wait_recv()
    marks_row = jnp.sum(mark_in[...], axis=0).astype(F32)
    spread = one_hot(iota((TOK, 16 * PEERS), 0) == iota((TOK, 16 * PEERS), 1) // 4)
    spread_row = dot(jnp.broadcast_to(marks_row, (8, TOK)).astype(BF16), spread)[0:1, :]
    codes_row = spread_row.astype(I32) + lax.rem(iota((1, 16 * PEERS), 1), 4) * 256
    tall = iota((4 * TOK, 1), 0)
    codes_col = lax.rem(tall, TOK) + 1 + tall // TOK * 256
    place[...] = one_hot(codes_col == codes_row)
    taken = jnp.sum(
        jnp.where((iota((TOK, TOK), 0) + 1).astype(F32) == marks_row, 1.0, 0.0),
        axis=1, keepdims=True,
    )
    image_mask[...] = jnp.broadcast_to(taken, (TOK, TOK))
    loads[5].wait()

    def mixed(landed, text_rows):
        return jnp.where(image_mask[...] > 0.0, landed, text_rows.astype(F32)).astype(BF16)

    def masked(rows):
        return jnp.where(image_mask[...] > 0.0, 0.0, rows).astype(BF16)

    def next_copy(g):
        return pltpu.make_async_remote_copy(
            src_ref=kv.at[g, 2 * TOK : 3 * TOK], dst_ref=kv.at[g, TOK : 2 * TOK],
            send_sem=kv_send.at[g], recv_sem=kv_recv.at[g],
            device_id=(e, l, up), device_id_type=MESH,
        )

    def relay_copy(g):
        return pltpu.make_async_remote_copy(
            src_ref=kv.at[g, TOK : 2 * TOK], dst_ref=kv.at[g, 0:TOK],
            send_sem=relay_send.at[g], recv_sem=relay_recv.at[g],
            device_id=(e, l, up), device_id_type=MESH,
        )

    def far_copy(g, t):
        return pltpu.make_async_remote_copy(
            src_ref=far.at[g, t], dst_ref=far_in.at[g, t],
            send_sem=far_send.at[g, t], recv_sem=far_recv.at[g, t],
            device_id=(e, l, down), device_id_type=MESH,
        )

    def pass_copy(g, t):
        return pltpu.make_async_remote_copy(
            src_ref=pass_out.at[g, t], dst_ref=pass_in.at[g, t],
            send_sem=pass_send.at[g, t], recv_sem=pass_recv.at[g, t],
            device_id=(e, l, down), device_id_type=MESH,
        )

    def relay(g):
        next_copy(g).wait_recv()
        relay_copy(g).start()

    def place_kv(t):
        whole(*kv_rows_of(t)).wait_recv()
        landed = dot(place[...], kv_rows_in[t].reshape(16 * PEERS, 128))
        for b in range(4):
            g, half = 2 * t + b // 2, b % 2
            kv[g, 2 * TOK : 3 * TOK, half * 128 : (half + 1) * 128] = mixed(
                landed[b * 128 : (b + 1) * 128], text[:, kv_columns(g, half)]
            )

    place_kv(0)
    next_copy(0).start()
    next_copy(1).start()
    place_kv(1)

    tall = iota((16 * PEERS, TOK), 0)
    spread_col = jnp.sum(
        jnp.where(iota((16 * PEERS, TOK), 1) == tall // 4, marks_row, 0.0),
        axis=1, keepdims=True,
    )
    codes_col = spread_col.astype(I32) + lax.rem(iota((16 * PEERS, 1), 0), 4) * 256
    wide = iota((1, 4 * TOK), 1)
    collect[...] = one_hot(codes_col == lax.rem(wide, TOK) + 1 + wide // TOK * 256)

    relay(0)
    next_copy(2).start()
    relay(1)
    next_copy(3).start()

    def chain(g):
        for t in (1, 0):
            far_copy(g, t).wait_recv()
            pass_out[g, t] = (near[g, t] + far_in[g, t].astype(F32)).astype(BF16)
            pass_copy(g, t).start()

    def finish(g):
        for t in (1, 0):
            pass_copy(g, t).wait_recv()
            kv_grad[g, t] = (own[g, t] + pass_in[g, t].astype(F32)).astype(BF16)

    loads[6].wait()

    def group(g, carry):
        whole(*rows_of(g)).wait_recv()
        arrived = jnp.concatenate(
            [row_in[g, :, t].reshape(16 * PEERS, 128) for t in range(2)], axis=1
        )
        landed = dot(place[...], arrived)
        for t in range(2):
            for b in range(4):
                h = t * 4 + b
                queries[h * 128 : (h + 1) * 128, :] = mixed(
                    landed[b * 128 : (b + 1) * 128, t * 128 : (t + 1) * 128],
                    text[:, q_columns(g, t, b)],
                )

        relay_copy(g).wait_recv()
        keys = kv[g, :, 0:128]
        values = kv[g, :, 128:256]
        cots = [
            cot[:, pl.ds(pl.multiple_of(g * PART + h * 128, 128), 128)] for h in range(GROUP)
        ]
        is_own = causal[...] > 0.0
        own_part = causal[...].astype(BF16)
        far_part = (1.0 - causal[...]).astype(BF16)

        def two_blocks(products):
            rest = jnp.where(is_own, products[2 * TOK :], products[0:TOK])
            return jnp.concatenate([rest, products[TOK : 2 * TOK]], axis=0)

        for pair in range(GROUP // 2):
            both = slice(pair * 256, (pair + 1) * 256)
            d_out = jnp.concatenate(cots[2 * pair : 2 * pair + 2], axis=0)
            logits = two_blocks(dot_t(keys, queries[both, :])) + bias[...]
            grad_probs = two_blocks(dot_t(values, d_out))
            top = jnp.max(logits, axis=0, keepdims=True)
            raised = jnp.exp2((logits - top) * EXP2_SCALE)
            inverse = 1.0 / jnp.sum(raised, axis=0, keepdims=True)
            delta = jnp.sum(raised * grad_probs, axis=0, keepdims=True) * inverse
            probs = (raised * inverse).astype(BF16)
            ds = (raised * ((grad_probs - delta) * (inverse * SCALE))).astype(BF16)
            for target, value in ((probs_t, probs), (ds_t, ds)):
                target[0:TOK, both] = value[0:TOK] * far_part
                target[TOK : 2 * TOK, both] = value[TOK : 2 * TOK]
                target[2 * TOK : 3 * TOK, both] = value[0:TOK] * own_part

        def pass_down(t, grad):
            far[g, t] = grad[0:TOK].astype(BF16)
            near[g, t] = grad[TOK : 2 * TOK]
            own[g, t] = grad[2 * TOK : 3 * TOK]
            far_copy(g, t).start()

        pass_down(1, dot(probs_t[...], jnp.concatenate(cots, axis=0)))
        pass_down(0, dot(ds_t[...], queries[...]))

        @pl.when(g < 2)
        def _():
            relay(g + 2)

        grads_t = dot(keys.T, ds_t[...]).astype(BF16)
        grads = [grads_t[:, h * 128 : (h + 1) * 128].T for h in range(GROUP)]
        gathered = dot(collect[...], four_tall(lambda t, b: grads[t * 4 + b], (0, 1)))
        gathered = gathered.astype(BF16)
        for t in range(2):
            grad_out[g, :, t] = gathered[:, t * 128 : (t + 1) * 128].reshape(PEERS, 16, 128)
        grad_in[g, pl.ds(me, 1)] = grad_out[g, pl.ds(me, 1)]
        scatter(*grads_of(g))

        @pl.when(g >= 1)
        def _():
            chain(g - 1)

        for t in range(2):
            for b in range(4):
                text_grad[:, q_columns(g, t, b)] = masked(grads[t * 4 + b].astype(F32))

        @pl.when(g >= 2)
        def _():
            finish(g - 2)

        return carry

    lax.fori_loop(0, KEY_VALUE_HEADS, group, 0)

    def return_kv(t):
        rows = four_tall(
            lambda _, b: kv_grad[2 * t + b // 2, b % 2], (0,)
        )
        kv_grads_out[t] = dot(collect[...], rows).astype(BF16).reshape(PEERS, 16, 128)
        kv_grads_in[t, pl.ds(me, 1)] = kv_grads_out[t, pl.ds(me, 1)]
        scatter(*kv_grads_of(t))

    def take_back(g, carry):
        whole(*grads_of(g)).wait_recv()
        returned = jnp.concatenate(
            [grad_in[g, :, t].reshape(16 * PEERS, 128) for t in range(2)], axis=1
        )
        back = dot(unpack[...], returned).astype(BF16)
        for t in range(2):
            for b in range(4):
                image_grad[:, q_columns(g, t, b)] = back[
                    b * IMG : (b + 1) * IMG, t * 128 : (t + 1) * 128
                ]
        return carry

    return_kv(0)
    chain(3)
    finish(2)
    take_back(0, 0)
    finish(3)
    return_kv(1)
    for g in range(KEY_VALUE_HEADS):
        for t in range(2):
            text_grad[:, kv_columns(g, t)] = masked(
                kv_grad[g, t].astype(F32)
            )
    lax.fori_loop(1, KEY_VALUE_HEADS, take_back, 0)

    whole(*marks_of).wait_send()
    for copy in seg_copies:
        copy.wait_send()

    def drain(g, carry):
        whole(*rows_of(g)).wait_send()
        whole(*grads_of(g)).wait_send()
        for copy in (next_copy, relay_copy):
            copy(g).wait_send()
        for t in range(2):
            far_copy(g, t).wait_send()
            pass_copy(g, t).wait_send()
        return carry

    lax.fori_loop(0, KEY_VALUE_HEADS, drain, 0)
    for t in range(2):
        whole(*kv_rows_of(t)).wait_send()
        whole(*kv_grads_of(t)).wait()
        back = dot(unpack[...], kv_grads_in[t].reshape(16 * PEERS, 128)).astype(BF16)
        for b in range(4):
            image_grad[:, kv_columns(2 * t + b // 2, b % 2)] = back[b * IMG : (b + 1) * IMG]


def write_out(text_grad, image_grad, text_out, image_out, sem):
    copies = [
        pltpu.make_async_copy(
            source.at[16 * n : 16 * n + 16], target.at[16 * n : 16 * n + 16], sem.at[i, n]
        )
        for i, (source, target) in enumerate(((text_grad, text_out), (image_grad, image_out)))
        for n in range(source.shape[0] // 16)
    ]
    for copy in copies:
        copy.start()
    for copy in copies:
        copy.wait()


def body(text_qkv, segments, image_qkv, patch_counts, image_dest, image_offset, output_cotangent):
    hbm = pl.BlockSpec(memory_space=pl.ANY)
    dma = pltpu.SemaphoreType.DMA
    q_cols = QUERY_HEADS * HEAD_SIZE
    tiles = (KEY_VALUE_HEADS, PEERS, 2, 16, 128)
    kv_tiles = (2, PEERS, 16, 128)
    vmem = pl.BlockSpec(memory_space=pltpu.VMEM)
    halo = (KEY_VALUE_HEADS, 2, TOK, 128)
    text_grad, image_grad = pl.pallas_call(
        kernel,
        name="slab",
        out_shape=(pltpu.VMEM((TOK, COLS), BF16), pltpu.VMEM((IMG, COLS), BF16)),
        in_specs=[pl.BlockSpec(memory_space=pltpu.HBM)] * 7,
        out_specs=(vmem, vmem),
        scratch_shapes=[
            pltpu.VMEM((TOK, COLS), BF16),
            pltpu.VMEM((1, TOK), I32),
            pltpu.VMEM((IMG, COLS), BF16),
            pltpu.VMEM((1, 2), I32),
            pltpu.VMEM((1, IMG), I32),
            pltpu.VMEM((1, IMG), I32),
            pltpu.VMEM((TOK, q_cols), BF16),
            pltpu.VMEM((PEERS, 1, TOK), I32),
            pltpu.VMEM((PEERS, 1, TOK), I32),
            pltpu.VMEM(tiles, BF16),
            pltpu.VMEM(tiles, BF16),
            pltpu.VMEM(tiles, BF16),
            pltpu.VMEM(tiles, BF16),
            pltpu.VMEM(kv_tiles, BF16),
            pltpu.VMEM(kv_tiles, BF16),
            pltpu.VMEM(kv_tiles, BF16),
            pltpu.VMEM(kv_tiles, BF16),
            pltpu.VMEM((2, 1, TOK), I32),
            pltpu.VMEM((16 * PEERS, 4 * IMG), BF16),
            pltpu.VMEM((4 * IMG, 16 * PEERS), BF16),
            pltpu.VMEM((4 * TOK, 16 * PEERS), BF16),
            pltpu.VMEM((16 * PEERS, 4 * TOK), BF16),
            pltpu.VMEM((2 * TOK, 256), F32),
            pltpu.VMEM((TOK, 256), F32),
            pltpu.VMEM((TOK, 128), F32),
            pltpu.VMEM((KEY_VALUE_HEADS, KEYS, 256), BF16),
            pltpu.VMEM((GROUP * TOK, 128), BF16),
            pltpu.VMEM((KEYS, GROUP * TOK), BF16),
            pltpu.VMEM((KEYS, GROUP * TOK), BF16),
            pltpu.VMEM(halo, BF16),
            pltpu.VMEM(halo, F32),
            pltpu.VMEM(halo, F32),
            pltpu.VMEM(halo, BF16),
            pltpu.VMEM(halo, BF16),
            pltpu.VMEM(halo, BF16),
            pltpu.VMEM(halo, BF16),
            dma((7,)),
            dma, dma,
            dma((PARTS,)), dma((PARTS,)), dma((PARTS,)), dma((PARTS,)),
            dma((2,)), dma((2,)),
            dma((4,)), dma((4,)), dma((4,)), dma((4,)),
            dma((4, 2)), dma((4, 2)), dma((4, 2)), dma((4, 2)),
        ],
        compiler_params=pltpu.CompilerParams(
            collective_id=0, has_side_effects=True, vmem_limit_bytes=58 << 20
        ),
        cost_estimate=pl.CostEstimate(
            flops=4 << 30, bytes_accessed=5 << 20, transcendentals=2 << 20
        ),
    )(
        text_qkv[0, 0], segments[0], image_qkv[0, 0, 0], patch_counts[0, 0],
        image_dest[0, 0], image_offset[0, 0], output_cotangent[0, 0],
    )
    text_grad, image_grad = pl.pallas_call(
        write_out,
        name="write_out",
        out_shape=(
            jax.ShapeDtypeStruct((TOK, COLS), BF16),
            jax.ShapeDtypeStruct((IMG, COLS), BF16),
        ),
        in_specs=[vmem, vmem],
        out_specs=(hbm, hbm),
        scratch_shapes=[dma((2, TOK // 16))],
        compiler_params=pltpu.CompilerParams(vmem_limit_bytes=4 << 20),
    )(text_grad, image_grad)
    return text_grad[None, None], image_grad[None, None, None]


def solution(mesh):
    rows = P("enc", "llm", "sp", None)
    deep = P("enc", "llm", "sp", None, None)
    return jax.shard_map(
        body, mesh=mesh,
        in_specs=(rows, P("enc", "llm", "sp"), deep, rows, rows, rows, rows),
        out_specs=(rows, deep), check_vma=False,
    )
```

```python
import jax
import jax.numpy as jnp
from jax import lax
from jax.experimental import pallas as pl
from jax.experimental.pallas import tpu as pltpu
from jax.sharding import PartitionSpec as P

QUERY_HEADS = 32
KEY_VALUE_HEADS = 4
HEAD_SIZE = 128
TOK = 128
IMG = 64
PATCHES = 32
N_ENC = 8
N_LLM = 4
N_SP = 16
PEERS = N_ENC * N_LLM
SLOTS = 4
COLS = (QUERY_HEADS + 2 * KEY_VALUE_HEADS) * HEAD_SIZE
GROUP = QUERY_HEADS // KEY_VALUE_HEADS
KEYS = 3 * TOK
PARTS = 6
PART = 1024
SCALE = HEAD_SIZE ** (-0.5)
EXP2_SCALE = SCALE * 1.4426950408889634
HIDDEN = -1e30

MESH = pl.DeviceIdType.MESH
F32 = jnp.float32
BF16 = jnp.bfloat16
I32 = jnp.int32


def iota(shape, dim):
    return lax.broadcasted_iota(I32, shape, dim)


def dot(a, b):
    return jnp.dot(a, b, preferred_element_type=F32)


def dot_t(a, b):
    return lax.dot_general(a, b, (((1,), (1,)), ((), ())), preferred_element_type=F32)


def as_column(row, size):
    eye = iota((size, size), 0) == iota((size, size), 1)
    return jnp.sum(jnp.where(eye, row, 0.0), axis=1, keepdims=True)


def one_hot(condition):
    return jnp.where(condition, 1.0, 0.0).astype(BF16)


def kernel(
    text_hbm, seg_hbm, img_hbm, count_hbm, dest_hbm, offset_hbm, cot_hbm,
    text_grad, image_grad,
    text, seg, img, count, dest, offset, cot,
    mark_out, mark_in, row_out, row_in, grad_out, grad_in,
    kv_rows_out, kv_rows_in, kv_grads_out, kv_grads_in, seg_in,
    pack, unpack, place, collect, bias, causal, image_mask,
    kv, queries, probs_t, ds_t, far, near, own, far_in, pass_out, pass_in, kv_grad,
    load_sem, mark_send, mark_recv, row_send, row_recv, grad_send, grad_recv,
    seg_send, seg_recv, kv_send, kv_recv, relay_send, relay_recv,
    far_send, far_recv, pass_send, pass_recv,
):
    e, l, s = lax.axis_index("enc"), lax.axis_index("llm"), lax.axis_index("sp")
    me = e * N_LLM + l
    up, up2, down, down2 = (lax.rem(s + d, N_SP) for d in (1, 2, N_SP - 1, N_SP - 2))

    loads = [
        pltpu.make_async_copy(src, dst, load_sem.at[i])
        for i, (src, dst) in enumerate(
            (
                (dest_hbm, dest), (offset_hbm, offset), (count_hbm, count), (seg_hbm, seg),
                (img_hbm, img), (text_hbm, text), (cot_hbm, cot),
            )
        )
    ]
    for load in loads:
        load.start()

    barrier = pltpu.get_barrier_semaphore()

    def peer(i):
        p = lax.rem(me + i, PEERS)
        return p, (p // N_LLM, lax.rem(p, N_LLM), s)

    def greet(i, carry):
        pl.semaphore_signal(barrier, inc=1, device_id=peer(i)[1], device_id_type=MESH)
        return carry

    lax.fori_loop(1, PEERS, greet, 0)
    for z in (down, down2, up):
        pl.semaphore_signal(barrier, inc=1, device_id=(e, l, z), device_id_type=MESH)

    for load in loads[:3]:
        load.wait()
    row_id = iota((1, IMG), 1)
    counts = jnp.where(row_id < PATCHES, count[:, 0:1], count[:, 1:2])
    live_row = lax.rem(row_id, PATCHES) < counts
    dest_row = jnp.where(live_row, dest[...], -1).astype(F32)
    dest_col = as_column(dest_row, IMG)
    offset_col = as_column(offset[...].astype(F32), IMG)
    same = (dest_col == dest_row) & (dest_row >= 0.0)
    lower = iota((IMG, IMG), 1) < iota((IMG, IMG), 0)
    higher = iota((IMG, IMG), 0) < iota((IMG, IMG), 1)
    rank_col = jnp.sum(jnp.where(same & lower, 1.0, 0.0), axis=1, keepdims=True)
    rank_row = jnp.sum(jnp.where(same & higher, 1.0, 0.0), axis=0, keepdims=True)
    slot_row = jnp.where(dest_row >= 0.0, dest_row * SLOTS + rank_row, -1.0)
    slot_col = jnp.where(dest_col >= 0.0, dest_col * SLOTS + rank_col, -1.0)
    repeat = one_hot(lax.rem(iota((IMG, 4 * IMG), 1), IMG) == iota((IMG, 4 * IMG), 0))
    slots_row = dot(jnp.broadcast_to(slot_row, (8, IMG)).astype(BF16), repeat)[0:1, :]
    codes_row = slots_row.astype(I32) * 4 + iota((1, 4 * IMG), 1) // IMG
    pack[...] = one_hot(iota((16 * PEERS, 4 * IMG), 0) == codes_row)
    to_whom = one_hot(iota((PEERS, IMG), 0).astype(F32) == dest_row)
    lane = iota((IMG, TOK), 1)
    marks_mine = jnp.where(
        lane.astype(F32) == (me * SLOTS).astype(F32) + rank_col, offset_col + 1.0, 0.0
    ).astype(BF16)
    marks = dot(to_whom, marks_mine).astype(I32)
    for d in range(PEERS):
        mark_out[d] = marks[d : d + 1, :]
    mark_in[pl.ds(me, 1)] = mark_out[pl.ds(me, 1)]

    def four_tall(read, tiles):
        return jnp.concatenate(
            [jnp.concatenate([read(t, b) for b in range(4)], axis=0) for t in tiles], axis=1
        )

    def q_columns(g, t, b):
        return pl.ds(pl.multiple_of(g * PART + t * 512 + b * 128, 128), 128)

    def kv_columns(g, t):
        return slice(4096 + t * 512 + g * 128, 4096 + t * 512 + g * 128 + 128)

    def pack_queries(g):
        packed = dot(pack[...], four_tall(lambda t, b: img[:, q_columns(g, t, b)], (0, 1)))
        packed = packed.astype(BF16)
        for t in range(2):
            row_out[g, :, t] = packed[:, t * 128 : (t + 1) * 128].reshape(PEERS, 16, 128)
        row_in[g, pl.ds(me, 1)] = row_out[g, pl.ds(me, 1)]

    def pack_kv():
        packed = dot(
            pack[...],
            four_tall(lambda t, b: img[:, kv_columns(2 * t + b // 2, b % 2)], (0, 1)),
        ).astype(BF16)
        for t in range(2):
            kv_rows_out[t] = packed[:, t * 128 : (t + 1) * 128].reshape(PEERS, 16, 128)
            kv_rows_in[t, pl.ds(me, 1)] = kv_rows_out[t, pl.ds(me, 1)]

    def scatter(source, target, send_sem, recv_sem):
        def copy_of(i):
            p, device = peer(i)
            return pltpu.make_async_remote_copy(
                src_ref=source.at[p], dst_ref=target.at[me], send_sem=send_sem,
                recv_sem=recv_sem, device_id=device, device_id_type=MESH,
            )

        def three(n, carry):
            for i in range(3):
                copy_of(n * 3 + i + 1).start()
            return carry

        lax.fori_loop(0, (PEERS - 1) // 3, three, 0)
        copy_of(PEERS - 1).start()

    def whole(source, target, send_sem, recv_sem):
        return pltpu.make_async_remote_copy(
            src_ref=source.at[0 : PEERS - 1], dst_ref=target.at[0 : PEERS - 1],
            send_sem=send_sem, recv_sem=recv_sem, device_id=(e, l, up), device_id_type=MESH,
        )

    def rows_of(g):
        return row_out.at[g], row_in.at[g], row_send.at[g], row_recv.at[g]

    def kv_rows_of(t):
        return kv_rows_out.at[t], kv_rows_in.at[t], row_send.at[4 + t], row_recv.at[4 + t]

    def grads_of(g):
        return grad_out.at[g], grad_in.at[g], grad_send.at[g], grad_recv.at[g]

    def kv_grads_of(t):
        return kv_grads_out.at[t], kv_grads_in.at[t], grad_send.at[4 + t], grad_recv.at[4 + t]

    marks_of = (mark_out, mark_in, mark_send, mark_recv)

    loads[4].wait()
    pack_kv()
    loads[3].wait()
    pl.semaphore_wait(barrier, PEERS + 2)
    scatter(*marks_of)
    scatter(*kv_rows_of(0))
    scatter(*kv_rows_of(1))
    seg_copies = [
        pltpu.make_async_remote_copy(
            src_ref=seg, dst_ref=seg_in.at[i], send_sem=seg_send.at[i], recv_sem=seg_recv.at[i],
            device_id=(e, l, z), device_id_type=MESH,
        )
        for i, z in enumerate((up, up2))
    ]
    for copy in seg_copies:
        copy.start()

    def send_queries(g, carry):
        pack_queries(g)
        scatter(*rows_of(g))
        return carry

    lax.fori_loop(0, KEY_VALUE_HEADS, send_queries, 0)

    slots_col = jnp.concatenate([slot_col] * 4, axis=0)
    codes_col = slots_col.astype(I32) * 4 + iota((4 * IMG, 1), 0) // IMG
    unpack[...] = one_hot(codes_col == iota((4 * IMG, 16 * PEERS), 1))

    for copy in seg_copies:
        copy.wait_recv()
    seg_row = seg[...].astype(F32)
    seg_near = jnp.where(s >= 1, as_column(seg_in[0].astype(F32), TOK), -1.0)
    seg_far = jnp.where(s >= 2, as_column(seg_in[1].astype(F32), TOK), -1.0)
    seg_own = as_column(seg_row, TOK)
    earlier = iota((TOK, TOK), 0) <= iota((TOK, TOK), 1)
    near_bias = jnp.where(seg_near == seg_row, 0.0, HIDDEN)
    rest_bias = jnp.where(jnp.where(earlier, seg_own, seg_far) == seg_row, 0.0, HIDDEN)
    for h in range(2):
        half = slice(h * 128, (h + 1) * 128)
        bias[0:TOK, half] = rest_bias
        bias[TOK : 2 * TOK, half] = near_bias
        causal[:, half] = jnp.where(earlier, 1.0, 0.0)

    whole(*marks_of).wait_recv()
    marks_row = jnp.sum(mark_in[...], axis=0).astype(F32)
    spread = one_hot(iota((TOK, 16 * PEERS), 0) == iota((TOK, 16 * PEERS), 1) // 4)
    spread_row = dot(jnp.broadcast_to(marks_row, (8, TOK)).astype(BF16), spread)[0:1, :]
    codes_row = spread_row.astype(I32) + lax.rem(iota((1, 16 * PEERS), 1), 4) * 256
    tall = iota((4 * TOK, 1), 0)
    codes_col = lax.rem(tall, TOK) + 1 + tall // TOK * 256
    place[...] = one_hot(codes_col == codes_row)
    taken = jnp.sum(
        jnp.where((iota((TOK, TOK), 0) + 1).astype(F32) == marks_row, 1.0, 0.0),
        axis=1, keepdims=True,
    )
    image_mask[...] = jnp.broadcast_to(taken, (TOK, TOK))
    loads[5].wait()

    def mixed(landed, text_rows):
        return jnp.where(image_mask[...] > 0.0, landed, text_rows.astype(F32)).astype(BF16)

    def masked(rows):
        return jnp.where(image_mask[...] > 0.0, 0.0, rows).astype(BF16)

    def next_copy(g):
        return pltpu.make_async_remote_copy(
            src_ref=kv.at[g, 2 * TOK : 3 * TOK], dst_ref=kv.at[g, TOK : 2 * TOK],
            send_sem=kv_send.at[g], recv_sem=kv_recv.at[g],
            device_id=(e, l, up), device_id_type=MESH,
        )

    def relay_copy(g):
        return pltpu.make_async_remote_copy(
            src_ref=kv.at[g, TOK : 2 * TOK], dst_ref=kv.at[g, 0:TOK],
            send_sem=relay_send.at[g], recv_sem=relay_recv.at[g],
            device_id=(e, l, up), device_id_type=MESH,
        )

    def far_copy(g):
        return pltpu.make_async_remote_copy(
            src_ref=far.at[g], dst_ref=far_in.at[g],
            send_sem=far_send.at[g], recv_sem=far_recv.at[g],
            device_id=(e, l, down), device_id_type=MESH,
        )

    def pass_copy(g):
        return pltpu.make_async_remote_copy(
            src_ref=pass_out.at[g], dst_ref=pass_in.at[g],
            send_sem=pass_send.at[g], recv_sem=pass_recv.at[g],
            device_id=(e, l, down), device_id_type=MESH,
        )

    def relay(g):
        next_copy(g).wait_recv()
        relay_copy(g).start()

    def place_kv(t):
        whole(*kv_rows_of(t)).wait_recv()
        landed = dot(place[...], kv_rows_in[t].reshape(16 * PEERS, 128))
        for b in range(4):
            g, half = 2 * t + b // 2, b % 2
            kv[g, 2 * TOK : 3 * TOK, half * 128 : (half + 1) * 128] = mixed(
                landed[b * 128 : (b + 1) * 128], text[:, kv_columns(g, half)]
            )

    place_kv(0)
    next_copy(0).start()
    place_kv(1)

    tall = iota((16 * PEERS, TOK), 0)
    spread_col = jnp.sum(
        jnp.where(iota((16 * PEERS, TOK), 1) == tall // 4, marks_row, 0.0),
        axis=1, keepdims=True,
    )
    codes_col = spread_col.astype(I32) + lax.rem(iota((16 * PEERS, 1), 0), 4) * 256
    wide = iota((1, 4 * TOK), 1)
    collect[...] = one_hot(codes_col == lax.rem(wide, TOK) + 1 + wide // TOK * 256)

    next_copy(1).start()
    relay(0)
    relay(1)
    next_copy(2).start()

    def chain(g):
        far_copy(g).wait_recv()
        pass_out[g] = (near[g] + far_in[g].astype(F32)).astype(BF16)
        pass_copy(g).start()

    def finish(g):
        pass_copy(g).wait_recv()
        kv_grad[g] = (own[g] + pass_in[g].astype(F32)).astype(BF16)

    loads[6].wait()

    def group(g, carry):
        whole(*rows_of(g)).wait_recv()
        arrived = jnp.concatenate(
            [row_in[g, :, t].reshape(16 * PEERS, 128) for t in range(2)], axis=1
        )
        landed = dot(place[...], arrived)
        for t in range(2):
            for b in range(4):
                h = t * 4 + b
                queries[h * 128 : (h + 1) * 128, :] = mixed(
                    landed[b * 128 : (b + 1) * 128, t * 128 : (t + 1) * 128],
                    text[:, q_columns(g, t, b)],
                )

        relay_copy(g).wait_recv()
        keys = kv[g, :, 0:128]
        values = kv[g, :, 128:256]
        cots = [
            cot[:, pl.ds(pl.multiple_of(g * PART + h * 128, 128), 128)] for h in range(GROUP)
        ]
        is_own = causal[...] > 0.0
        own_part = causal[...].astype(BF16)
        far_part = (1.0 - causal[...]).astype(BF16)

        def two_blocks(products):
            rest = jnp.where(is_own, products[2 * TOK :], products[0:TOK])
            return jnp.concatenate([rest, products[TOK : 2 * TOK]], axis=0)

        for pair in range(GROUP // 2):
            both = slice(pair * 256, (pair + 1) * 256)
            d_out = jnp.concatenate(cots[2 * pair : 2 * pair + 2], axis=0)
            logits = two_blocks(dot_t(keys, queries[both, :])) + bias[...]
            grad_probs = two_blocks(dot_t(values, d_out))
            top = jnp.max(logits, axis=0, keepdims=True)
            raised = jnp.exp2((logits - top) * EXP2_SCALE)
            inverse = 1.0 / jnp.sum(raised, axis=0, keepdims=True)
            delta = jnp.sum(raised * grad_probs, axis=0, keepdims=True) * inverse
            probs = (raised * inverse).astype(BF16)
            ds = (raised * ((grad_probs - delta) * (inverse * SCALE))).astype(BF16)
            for target, value in ((probs_t, probs), (ds_t, ds)):
                target[0:TOK, both] = value[0:TOK] * far_part
                target[TOK : 2 * TOK, both] = value[TOK : 2 * TOK]
                target[2 * TOK : 3 * TOK, both] = value[0:TOK] * own_part
        key_grad = dot(ds_t[...], queries[...])
        value_grad = dot(probs_t[...], jnp.concatenate(cots, axis=0))
        for t, grad in enumerate((key_grad, value_grad)):
            half = slice(t * 128, (t + 1) * 128)
            far[g, :, half] = grad[0:TOK].astype(BF16)
            near[g, :, half] = grad[TOK : 2 * TOK]
            own[g, :, half] = grad[2 * TOK : 3 * TOK]
        far_copy(g).start()

        @pl.when(g == 0)
        def _():
            next_copy(3).start()

        grads_t = dot(keys.T, ds_t[...]).astype(BF16)
        grads = [grads_t[:, h * 128 : (h + 1) * 128].T for h in range(GROUP)]
        gathered = dot(collect[...], four_tall(lambda t, b: grads[t * 4 + b], (0, 1)))
        gathered = gathered.astype(BF16)
        for t in range(2):
            grad_out[g, :, t] = gathered[:, t * 128 : (t + 1) * 128].reshape(PEERS, 16, 128)
        grad_in[g, pl.ds(me, 1)] = grad_out[g, pl.ds(me, 1)]
        scatter(*grads_of(g))

        @pl.when(g >= 1)
        def _():
            chain(g - 1)

        for t in range(2):
            for b in range(4):
                text_grad[:, q_columns(g, t, b)] = masked(grads[t * 4 + b].astype(F32))

        @pl.when(g < 2)
        def _():
            relay(g + 2)

        @pl.when(g >= 2)
        def _():
            finish(g - 2)

        return carry

    lax.fori_loop(0, KEY_VALUE_HEADS, group, 0)

    def return_kv(t):
        rows = four_tall(
            lambda _, b: kv_grad[2 * t + b // 2, :, b % 2 * 128 : (b % 2 + 1) * 128], (0,)
        )
        kv_grads_out[t] = dot(collect[...], rows).astype(BF16).reshape(PEERS, 16, 128)
        kv_grads_in[t, pl.ds(me, 1)] = kv_grads_out[t, pl.ds(me, 1)]
        scatter(*kv_grads_of(t))

    def take_back(g, carry):
        whole(*grads_of(g)).wait_recv()
        returned = jnp.concatenate(
            [grad_in[g, :, t].reshape(16 * PEERS, 128) for t in range(2)], axis=1
        )
        back = dot(unpack[...], returned).astype(BF16)
        for t in range(2):
            for b in range(4):
                image_grad[:, q_columns(g, t, b)] = back[
                    b * IMG : (b + 1) * IMG, t * 128 : (t + 1) * 128
                ]
        return carry

    return_kv(0)
    chain(3)
    finish(2)
    take_back(0, 0)
    finish(3)
    return_kv(1)
    for g in range(KEY_VALUE_HEADS):
        for t in range(2):
            text_grad[:, kv_columns(g, t)] = masked(
                kv_grad[g, :, t * 128 : (t + 1) * 128].astype(F32)
            )
    lax.fori_loop(1, KEY_VALUE_HEADS, take_back, 0)

    whole(*marks_of).wait_send()
    for copy in seg_copies:
        copy.wait_send()

    def drain(g, carry):
        whole(*rows_of(g)).wait_send()
        whole(*grads_of(g)).wait_send()
        for copy in (next_copy, relay_copy, far_copy, pass_copy):
            copy(g).wait_send()
        return carry

    lax.fori_loop(0, KEY_VALUE_HEADS, drain, 0)
    for t in range(2):
        whole(*kv_rows_of(t)).wait_send()
        whole(*kv_grads_of(t)).wait()
        back = dot(unpack[...], kv_grads_in[t].reshape(16 * PEERS, 128)).astype(BF16)
        for b in range(4):
            image_grad[:, kv_columns(2 * t + b // 2, b % 2)] = back[b * IMG : (b + 1) * IMG]


def write_out(text_grad, image_grad, text_out, image_out, sem):
    copies = [
        pltpu.make_async_copy(text_grad, text_out, sem.at[0]),
        pltpu.make_async_copy(image_grad, image_out, sem.at[1]),
    ]
    for copy in copies:
        copy.start()
    for copy in copies:
        copy.wait()


def body(text_qkv, segments, image_qkv, patch_counts, image_dest, image_offset, output_cotangent):
    hbm = pl.BlockSpec(memory_space=pl.ANY)
    dma = pltpu.SemaphoreType.DMA
    q_cols = QUERY_HEADS * HEAD_SIZE
    tiles = (KEY_VALUE_HEADS, PEERS, 2, 16, 128)
    kv_tiles = (2, PEERS, 16, 128)
    vmem = pl.BlockSpec(memory_space=pltpu.VMEM)
    halo = (KEY_VALUE_HEADS, TOK, 256)
    text_grad, image_grad = pl.pallas_call(
        kernel,
        name="slab",
        out_shape=(pltpu.VMEM((TOK, COLS), BF16), pltpu.VMEM((IMG, COLS), BF16)),
        in_specs=[pl.BlockSpec(memory_space=pltpu.HBM)] * 7,
        out_specs=(vmem, vmem),
        scratch_shapes=[
            pltpu.VMEM((TOK, COLS), BF16),
            pltpu.VMEM((1, TOK), I32),
            pltpu.VMEM((IMG, COLS), BF16),
            pltpu.VMEM((1, 2), I32),
            pltpu.VMEM((1, IMG), I32),
            pltpu.VMEM((1, IMG), I32),
            pltpu.VMEM((TOK, q_cols), BF16),
            pltpu.VMEM((PEERS, 1, TOK), I32),
            pltpu.VMEM((PEERS, 1, TOK), I32),
            pltpu.VMEM(tiles, BF16),
            pltpu.VMEM(tiles, BF16),
            pltpu.VMEM(tiles, BF16),
            pltpu.VMEM(tiles, BF16),
            pltpu.VMEM(kv_tiles, BF16),
            pltpu.VMEM(kv_tiles, BF16),
            pltpu.VMEM(kv_tiles, BF16),
            pltpu.VMEM(kv_tiles, BF16),
            pltpu.VMEM((2, 1, TOK), I32),
            pltpu.VMEM((16 * PEERS, 4 * IMG), BF16),
            pltpu.VMEM((4 * IMG, 16 * PEERS), BF16),
            pltpu.VMEM((4 * TOK, 16 * PEERS), BF16),
            pltpu.VMEM((16 * PEERS, 4 * TOK), BF16),
            pltpu.VMEM((2 * TOK, 256), F32),
            pltpu.VMEM((TOK, 256), F32),
            pltpu.VMEM((TOK, 128), F32),
            pltpu.VMEM((KEY_VALUE_HEADS, KEYS, 256), BF16),
            pltpu.VMEM((GROUP * TOK, 128), BF16),
            pltpu.VMEM((KEYS, GROUP * TOK), BF16),
            pltpu.VMEM((KEYS, GROUP * TOK), BF16),
            pltpu.VMEM(halo, BF16),
            pltpu.VMEM(halo, F32),
            pltpu.VMEM(halo, F32),
            pltpu.VMEM(halo, BF16),
            pltpu.VMEM(halo, BF16),
            pltpu.VMEM(halo, BF16),
            pltpu.VMEM(halo, BF16),
            dma((7,)),
            dma, dma,
            dma((PARTS,)), dma((PARTS,)), dma((PARTS,)), dma((PARTS,)),
            dma((2,)), dma((2,)),
            dma((4,)), dma((4,)), dma((4,)), dma((4,)),
            dma((4,)), dma((4,)), dma((4,)), dma((4,)),
        ],
        compiler_params=pltpu.CompilerParams(
            collective_id=0, has_side_effects=True, vmem_limit_bytes=58 << 20
        ),
        cost_estimate=pl.CostEstimate(
            flops=4 << 30, bytes_accessed=5 << 20, transcendentals=2 << 20
        ),
    )(
        text_qkv[0, 0], segments[0], image_qkv[0, 0, 0], patch_counts[0, 0],
        image_dest[0, 0], image_offset[0, 0], output_cotangent[0, 0],
    )
    text_grad, image_grad = pl.pallas_call(
        write_out,
        name="write_out",
        out_shape=(
            jax.ShapeDtypeStruct((TOK, COLS), BF16),
            jax.ShapeDtypeStruct((IMG, COLS), BF16),
        ),
        in_specs=[vmem, vmem],
        out_specs=(hbm, hbm),
        scratch_shapes=[dma((2,))],
        compiler_params=pltpu.CompilerParams(vmem_limit_bytes=4 << 20),
    )(text_grad, image_grad)
    return text_grad[None, None], image_grad[None, None, None]


def solution(mesh):
    rows = P("enc", "llm", "sp", None)
    deep = P("enc", "llm", "sp", None, None)
    return jax.shard_map(
        body, mesh=mesh,
        in_specs=(rows, P("enc", "llm", "sp"), deep, rows, rows, rows, rows),
        out_specs=(rows, deep), check_vma=False,
    )
```

```python
import jax
import jax.numpy as jnp
from jax import lax
from jax.experimental import pallas as pl
from jax.experimental.pallas import tpu as pltpu
from jax.sharding import PartitionSpec as P

QUERY_HEADS = 32
KEY_VALUE_HEADS = 4
HEAD_SIZE = 128
TOK = 128
IMG = 64
PATCHES = 32
N_ENC = 8
N_LLM = 4
N_SP = 16
PEERS = N_ENC * N_LLM
SLOTS = 4
COLS = (QUERY_HEADS + 2 * KEY_VALUE_HEADS) * HEAD_SIZE
GROUP = QUERY_HEADS // KEY_VALUE_HEADS
KEYS = 3 * TOK
PARTS = 6
PART = 1024
SCALE = HEAD_SIZE ** (-0.5)
EXP2_SCALE = SCALE * 1.4426950408889634
HIDDEN = -1e30

MESH = pl.DeviceIdType.MESH
F32 = jnp.float32
BF16 = jnp.bfloat16
I32 = jnp.int32


def iota(shape, dim):
    return lax.broadcasted_iota(I32, shape, dim)


def dot(a, b):
    return jnp.dot(a, b, preferred_element_type=F32)


def dot_t(a, b):
    return lax.dot_general(a, b, (((1,), (1,)), ((), ())), preferred_element_type=F32)


def as_column(row, size):
    eye = iota((size, size), 0) == iota((size, size), 1)
    return jnp.sum(jnp.where(eye, row, 0.0), axis=1, keepdims=True)


def one_hot(condition):
    return jnp.where(condition, 1.0, 0.0).astype(BF16)


def kernel(
    text_hbm, seg_hbm, img_hbm, count_hbm, dest_hbm, offset_hbm, cot_hbm,
    text_grad, image_grad,
    text, seg, img, count, dest, offset, cot,
    mark_out, mark_in, row_out, row_in, grad_out, grad_in,
    kv_rows_out, kv_rows_in, kv_grads_out, kv_grads_in, seg_in,
    pack, unpack, place, collect, bias, causal, image_mask,
    kv, queries, probs_t, ds_t, far, near, own, far_in, pass_out, pass_in, kv_grad,
    load_sem, mark_send, mark_recv, row_send, row_recv, grad_send, grad_recv,
    seg_send, seg_recv, kv_send, kv_recv, relay_send, relay_recv,
    far_send, far_recv, pass_send, pass_recv,
):
    e, l, s = lax.axis_index("enc"), lax.axis_index("llm"), lax.axis_index("sp")
    me = e * N_LLM + l
    up, up2, down, down2 = (lax.rem(s + d, N_SP) for d in (1, 2, N_SP - 1, N_SP - 2))

    loads = [
        pltpu.make_async_copy(src, dst, load_sem.at[i])
        for i, (src, dst) in enumerate(
            (
                (dest_hbm, dest), (offset_hbm, offset), (count_hbm, count), (seg_hbm, seg),
                (img_hbm, img), (text_hbm, text), (cot_hbm, cot),
            )
        )
    ]
    for load in loads:
        load.start()

    barrier = pltpu.get_barrier_semaphore()

    def peer(i):
        p = lax.rem(me + i, PEERS)
        return p, (p // N_LLM, lax.rem(p, N_LLM), s)

    def greet(i, carry):
        pl.semaphore_signal(barrier, inc=1, device_id=peer(i)[1], device_id_type=MESH)
        return carry

    lax.fori_loop(1, PEERS, greet, 0)
    for z in (down, down2, up):
        pl.semaphore_signal(barrier, inc=1, device_id=(e, l, z), device_id_type=MESH)

    for load in loads[:3]:
        load.wait()
    row_id = iota((1, IMG), 1)
    counts = jnp.where(row_id < PATCHES, count[:, 0:1], count[:, 1:2])
    live_row = lax.rem(row_id, PATCHES) < counts
    dest_row = jnp.where(live_row, dest[...], -1).astype(F32)
    dest_col = as_column(dest_row, IMG)
    offset_col = as_column(offset[...].astype(F32), IMG)
    same = (dest_col == dest_row) & (dest_row >= 0.0)
    lower = iota((IMG, IMG), 1) < iota((IMG, IMG), 0)
    higher = iota((IMG, IMG), 0) < iota((IMG, IMG), 1)
    rank_col = jnp.sum(jnp.where(same & lower, 1.0, 0.0), axis=1, keepdims=True)
    rank_row = jnp.sum(jnp.where(same & higher, 1.0, 0.0), axis=0, keepdims=True)
    slot_row = jnp.where(dest_row >= 0.0, dest_row * SLOTS + rank_row, -1.0)
    slot_col = jnp.where(dest_col >= 0.0, dest_col * SLOTS + rank_col, -1.0)
    repeat = one_hot(lax.rem(iota((IMG, 4 * IMG), 1), IMG) == iota((IMG, 4 * IMG), 0))
    slots_row = dot(jnp.broadcast_to(slot_row, (8, IMG)).astype(BF16), repeat)[0:1, :]
    codes_row = slots_row.astype(I32) * 4 + iota((1, 4 * IMG), 1) // IMG
    pack[...] = one_hot(iota((16 * PEERS, 4 * IMG), 0) == codes_row)
    to_whom = one_hot(iota((PEERS, IMG), 0).astype(F32) == dest_row)
    lane = iota((IMG, TOK), 1)
    marks_mine = jnp.where(
        lane.astype(F32) == (me * SLOTS).astype(F32) + rank_col, offset_col + 1.0, 0.0
    ).astype(BF16)
    marks = dot(to_whom, marks_mine).astype(I32)
    for d in range(PEERS):
        mark_out[d] = marks[d : d + 1, :]
    mark_in[pl.ds(me, 1)] = mark_out[pl.ds(me, 1)]

    def four_tall(read, tiles):
        return jnp.concatenate(
            [jnp.concatenate([read(t, b) for b in range(4)], axis=0) for t in tiles], axis=1
        )

    def q_columns(g, t, b):
        return pl.ds(pl.multiple_of(g * PART + t * 512 + b * 128, 128), 128)

    def kv_columns(g, t):
        return slice(4096 + t * 512 + g * 128, 4096 + t * 512 + g * 128 + 128)

    def pack_queries(g):
        packed = dot(pack[...], four_tall(lambda t, b: img[:, q_columns(g, t, b)], (0, 1)))
        packed = packed.astype(BF16)
        for t in range(2):
            row_out[g, :, t] = packed[:, t * 128 : (t + 1) * 128].reshape(PEERS, 16, 128)
        row_in[g, pl.ds(me, 1)] = row_out[g, pl.ds(me, 1)]

    def pack_kv():
        packed = dot(
            pack[...],
            four_tall(lambda t, b: img[:, kv_columns(2 * t + b // 2, b % 2)], (0, 1)),
        ).astype(BF16)
        for t in range(2):
            kv_rows_out[t] = packed[:, t * 128 : (t + 1) * 128].reshape(PEERS, 16, 128)
            kv_rows_in[t, pl.ds(me, 1)] = kv_rows_out[t, pl.ds(me, 1)]

    def scatter(source, target, send_sem, recv_sem):
        def copy_of(i):
            p, device = peer(i)
            return pltpu.make_async_remote_copy(
                src_ref=source.at[p], dst_ref=target.at[me], send_sem=send_sem,
                recv_sem=recv_sem, device_id=device, device_id_type=MESH,
            )

        def two(n, carry):
            copy_of(PEERS // 2 - n).start()
            copy_of(PEERS // 2 + n).start()
            return carry

        copy_of(PEERS // 2).start()
        lax.fori_loop(1, PEERS // 2, two, 0)

    def whole(source, target, send_sem, recv_sem):
        return pltpu.make_async_remote_copy(
            src_ref=source.at[0 : PEERS - 1], dst_ref=target.at[0 : PEERS - 1],
            send_sem=send_sem, recv_sem=recv_sem, device_id=(e, l, up), device_id_type=MESH,
        )

    def rows_of(g):
        return row_out.at[g], row_in.at[g], row_send.at[g], row_recv.at[g]

    def kv_rows_of(t):
        return kv_rows_out.at[t], kv_rows_in.at[t], row_send.at[4 + t], row_recv.at[4 + t]

    def grads_of(g):
        return grad_out.at[g], grad_in.at[g], grad_send.at[g], grad_recv.at[g]

    def kv_grads_of(t):
        return kv_grads_out.at[t], kv_grads_in.at[t], grad_send.at[4 + t], grad_recv.at[4 + t]

    marks_of = (mark_out, mark_in, mark_send, mark_recv)

    loads[4].wait()
    pack_kv()
    loads[3].wait()
    pl.semaphore_wait(barrier, PEERS + 2)
    scatter(*marks_of)
    scatter(*kv_rows_of(0))
    scatter(*kv_rows_of(1))
    seg_copies = [
        pltpu.make_async_remote_copy(
            src_ref=seg, dst_ref=seg_in.at[i], send_sem=seg_send.at[i], recv_sem=seg_recv.at[i],
            device_id=(e, l, z), device_id_type=MESH,
        )
        for i, z in enumerate((up, up2))
    ]
    for copy in seg_copies:
        copy.start()

    def send_queries(g, carry):
        pack_queries(g)
        scatter(*rows_of(g))
        return carry

    lax.fori_loop(0, KEY_VALUE_HEADS, send_queries, 0)

    slots_col = jnp.concatenate([slot_col] * 4, axis=0)
    codes_col = slots_col.astype(I32) * 4 + iota((4 * IMG, 1), 0) // IMG
    unpack[...] = one_hot(codes_col == iota((4 * IMG, 16 * PEERS), 1))

    for copy in seg_copies:
        copy.wait_recv()
    seg_row = seg[...].astype(F32)
    seg_near = jnp.where(s >= 1, as_column(seg_in[0].astype(F32), TOK), -1.0)
    seg_far = jnp.where(s >= 2, as_column(seg_in[1].astype(F32), TOK), -1.0)
    seg_own = as_column(seg_row, TOK)
    earlier = iota((TOK, TOK), 0) <= iota((TOK, TOK), 1)
    near_bias = jnp.where(seg_near == seg_row, 0.0, HIDDEN)
    rest_bias = jnp.where(jnp.where(earlier, seg_own, seg_far) == seg_row, 0.0, HIDDEN)
    for h in range(2):
        half = slice(h * 128, (h + 1) * 128)
        bias[0:TOK, half] = rest_bias
        bias[TOK : 2 * TOK, half] = near_bias
        causal[:, half] = jnp.where(earlier, 1.0, 0.0)

    whole(*marks_of).wait_recv()
    marks_row = jnp.sum(mark_in[...], axis=0).astype(F32)
    spread = one_hot(iota((TOK, 16 * PEERS), 0) == iota((TOK, 16 * PEERS), 1) // 4)
    spread_row = dot(jnp.broadcast_to(marks_row, (8, TOK)).astype(BF16), spread)[0:1, :]
    codes_row = spread_row.astype(I32) + lax.rem(iota((1, 16 * PEERS), 1), 4) * 256
    tall = iota((4 * TOK, 1), 0)
    codes_col = lax.rem(tall, TOK) + 1 + tall // TOK * 256
    place[...] = one_hot(codes_col == codes_row)
    taken = jnp.sum(
        jnp.where((iota((TOK, TOK), 0) + 1).astype(F32) == marks_row, 1.0, 0.0),
        axis=1, keepdims=True,
    )
    image_mask[...] = jnp.broadcast_to(taken, (TOK, TOK))
    loads[5].wait()

    def mixed(landed, text_rows):
        return jnp.where(image_mask[...] > 0.0, landed, text_rows.astype(F32)).astype(BF16)

    def masked(rows):
        return jnp.where(image_mask[...] > 0.0, 0.0, rows).astype(BF16)

    def next_copy(g):
        return pltpu.make_async_remote_copy(
            src_ref=kv.at[g, 2 * TOK : 3 * TOK], dst_ref=kv.at[g, TOK : 2 * TOK],
            send_sem=kv_send.at[g], recv_sem=kv_recv.at[g],
            device_id=(e, l, up), device_id_type=MESH,
        )

    def relay_copy(g):
        return pltpu.make_async_remote_copy(
            src_ref=kv.at[g, TOK : 2 * TOK], dst_ref=kv.at[g, 0:TOK],
            send_sem=relay_send.at[g], recv_sem=relay_recv.at[g],
            device_id=(e, l, up), device_id_type=MESH,
        )

    def far_copy(g):
        return pltpu.make_async_remote_copy(
            src_ref=far.at[g], dst_ref=far_in.at[g],
            send_sem=far_send.at[g], recv_sem=far_recv.at[g],
            device_id=(e, l, down), device_id_type=MESH,
        )

    def pass_copy(g):
        return pltpu.make_async_remote_copy(
            src_ref=pass_out.at[g], dst_ref=pass_in.at[g],
            send_sem=pass_send.at[g], recv_sem=pass_recv.at[g],
            device_id=(e, l, down), device_id_type=MESH,
        )

    def relay(g):
        next_copy(g).wait_recv()
        relay_copy(g).start()

    def place_kv(t):
        whole(*kv_rows_of(t)).wait_recv()
        landed = dot(place[...], kv_rows_in[t].reshape(16 * PEERS, 128))
        for b in range(4):
            g, half = 2 * t + b // 2, b % 2
            kv[g, 2 * TOK : 3 * TOK, half * 128 : (half + 1) * 128] = mixed(
                landed[b * 128 : (b + 1) * 128], text[:, kv_columns(g, half)]
            )

    place_kv(0)
    next_copy(0).start()
    next_copy(1).start()
    place_kv(1)

    tall = iota((16 * PEERS, TOK), 0)
    spread_col = jnp.sum(
        jnp.where(iota((16 * PEERS, TOK), 1) == tall // 4, marks_row, 0.0),
        axis=1, keepdims=True,
    )
    codes_col = spread_col.astype(I32) + lax.rem(iota((16 * PEERS, 1), 0), 4) * 256
    wide = iota((1, 4 * TOK), 1)
    collect[...] = one_hot(codes_col == lax.rem(wide, TOK) + 1 + wide // TOK * 256)

    relay(0)
    next_copy(2).start()
    relay(1)
    next_copy(3).start()

    def chain(g):
        far_copy(g).wait_recv()
        pass_out[g] = (near[g] + far_in[g].astype(F32)).astype(BF16)
        pass_copy(g).start()

    def finish(g):
        pass_copy(g).wait_recv()
        kv_grad[g] = (own[g] + pass_in[g].astype(F32)).astype(BF16)

    loads[6].wait()

    def group(g, carry):
        whole(*rows_of(g)).wait_recv()
        arrived = jnp.concatenate(
            [row_in[g, :, t].reshape(16 * PEERS, 128) for t in range(2)], axis=1
        )
        landed = dot(place[...], arrived)
        for t in range(2):
            for b in range(4):
                h = t * 4 + b
                queries[h * 128 : (h + 1) * 128, :] = mixed(
                    landed[b * 128 : (b + 1) * 128, t * 128 : (t + 1) * 128],
                    text[:, q_columns(g, t, b)],
                )

        relay_copy(g).wait_recv()
        keys = kv[g, :, 0:128]
        values = kv[g, :, 128:256]
        cots = [
            cot[:, pl.ds(pl.multiple_of(g * PART + h * 128, 128), 128)] for h in range(GROUP)
        ]
        is_own = causal[...] > 0.0
        own_part = causal[...].astype(BF16)
        far_part = (1.0 - causal[...]).astype(BF16)

        def two_blocks(products):
            rest = jnp.where(is_own, products[2 * TOK :], products[0:TOK])
            return jnp.concatenate([rest, products[TOK : 2 * TOK]], axis=0)

        for pair in range(GROUP // 2):
            both = slice(pair * 256, (pair + 1) * 256)
            d_out = jnp.concatenate(cots[2 * pair : 2 * pair + 2], axis=0)
            logits = two_blocks(dot_t(keys, queries[both, :])) + bias[...]
            grad_probs = two_blocks(dot_t(values, d_out))
            top = jnp.max(logits, axis=0, keepdims=True)
            raised = jnp.exp2((logits - top) * EXP2_SCALE)
            inverse = 1.0 / jnp.sum(raised, axis=0, keepdims=True)
            delta = jnp.sum(raised * grad_probs, axis=0, keepdims=True) * inverse
            probs = (raised * inverse).astype(BF16)
            ds = (raised * ((grad_probs - delta) * (inverse * SCALE))).astype(BF16)
            for target, value in ((probs_t, probs), (ds_t, ds)):
                target[0:TOK, both] = value[0:TOK] * far_part
                target[TOK : 2 * TOK, both] = value[TOK : 2 * TOK]
                target[2 * TOK : 3 * TOK, both] = value[0:TOK] * own_part
        key_grad = dot(ds_t[...], queries[...])
        value_grad = dot(probs_t[...], jnp.concatenate(cots, axis=0))
        for t, grad in enumerate((key_grad, value_grad)):
            half = slice(t * 128, (t + 1) * 128)
            far[g, :, half] = grad[0:TOK].astype(BF16)
            near[g, :, half] = grad[TOK : 2 * TOK]
            own[g, :, half] = grad[2 * TOK : 3 * TOK]
        far_copy(g).start()

        @pl.when(g < 2)
        def _():
            relay(g + 2)

        grads_t = dot(keys.T, ds_t[...]).astype(BF16)
        grads = [grads_t[:, h * 128 : (h + 1) * 128].T for h in range(GROUP)]
        gathered = dot(collect[...], four_tall(lambda t, b: grads[t * 4 + b], (0, 1)))
        gathered = gathered.astype(BF16)
        for t in range(2):
            grad_out[g, :, t] = gathered[:, t * 128 : (t + 1) * 128].reshape(PEERS, 16, 128)
        grad_in[g, pl.ds(me, 1)] = grad_out[g, pl.ds(me, 1)]
        scatter(*grads_of(g))

        @pl.when(g >= 1)
        def _():
            chain(g - 1)

        for t in range(2):
            for b in range(4):
                text_grad[:, q_columns(g, t, b)] = masked(grads[t * 4 + b].astype(F32))

        @pl.when(g >= 2)
        def _():
            finish(g - 2)

        return carry

    lax.fori_loop(0, KEY_VALUE_HEADS, group, 0)

    def return_kv(t):
        rows = four_tall(
            lambda _, b: kv_grad[2 * t + b // 2, :, b % 2 * 128 : (b % 2 + 1) * 128], (0,)
        )
        kv_grads_out[t] = dot(collect[...], rows).astype(BF16).reshape(PEERS, 16, 128)
        kv_grads_in[t, pl.ds(me, 1)] = kv_grads_out[t, pl.ds(me, 1)]
        scatter(*kv_grads_of(t))

    def take_back(g, carry):
        whole(*grads_of(g)).wait_recv()
        returned = jnp.concatenate(
            [grad_in[g, :, t].reshape(16 * PEERS, 128) for t in range(2)], axis=1
        )
        back = dot(unpack[...], returned).astype(BF16)
        for t in range(2):
            for b in range(4):
                image_grad[:, q_columns(g, t, b)] = back[
                    b * IMG : (b + 1) * IMG, t * 128 : (t + 1) * 128
                ]
        return carry

    return_kv(0)
    chain(3)
    finish(2)
    finish(3)
    return_kv(1)
    for g in range(KEY_VALUE_HEADS):
        for t in range(2):
            text_grad[:, kv_columns(g, t)] = masked(
                kv_grad[g, :, t * 128 : (t + 1) * 128].astype(F32)
            )
    lax.fori_loop(0, KEY_VALUE_HEADS, take_back, 0)

    whole(*marks_of).wait_send()
    for copy in seg_copies:
        copy.wait_send()

    def drain(g, carry):
        whole(*rows_of(g)).wait_send()
        whole(*grads_of(g)).wait_send()
        for copy in (next_copy, relay_copy, far_copy, pass_copy):
            copy(g).wait_send()
        return carry

    lax.fori_loop(0, KEY_VALUE_HEADS, drain, 0)
    for t in range(2):
        whole(*kv_rows_of(t)).wait_send()
        whole(*kv_grads_of(t)).wait()
        back = dot(unpack[...], kv_grads_in[t].reshape(16 * PEERS, 128)).astype(BF16)
        for b in range(4):
            image_grad[:, kv_columns(2 * t + b // 2, b % 2)] = back[b * IMG : (b + 1) * IMG]


def write_out(text_grad, image_grad, text_out, image_out, sem):
    copies = [
        pltpu.make_async_copy(text_grad, text_out, sem.at[0]),
        pltpu.make_async_copy(image_grad, image_out, sem.at[1]),
    ]
    for copy in copies:
        copy.start()
    for copy in copies:
        copy.wait()


def body(text_qkv, segments, image_qkv, patch_counts, image_dest, image_offset, output_cotangent):
    hbm = pl.BlockSpec(memory_space=pl.ANY)
    dma = pltpu.SemaphoreType.DMA
    q_cols = QUERY_HEADS * HEAD_SIZE
    tiles = (KEY_VALUE_HEADS, PEERS, 2, 16, 128)
    kv_tiles = (2, PEERS, 16, 128)
    vmem = pl.BlockSpec(memory_space=pltpu.VMEM)
    halo = (KEY_VALUE_HEADS, TOK, 256)
    text_grad, image_grad = pl.pallas_call(
        kernel,
        name="slab",
        out_shape=(pltpu.VMEM((TOK, COLS), BF16), pltpu.VMEM((IMG, COLS), BF16)),
        in_specs=[pl.BlockSpec(memory_space=pltpu.HBM)] * 7,
        out_specs=(vmem, vmem),
        scratch_shapes=[
            pltpu.VMEM((TOK, COLS), BF16),
            pltpu.VMEM((1, TOK), I32),
            pltpu.VMEM((IMG, COLS), BF16),
            pltpu.VMEM((1, 2), I32),
            pltpu.VMEM((1, IMG), I32),
            pltpu.VMEM((1, IMG), I32),
            pltpu.VMEM((TOK, q_cols), BF16),
            pltpu.VMEM((PEERS, 1, TOK), I32),
            pltpu.VMEM((PEERS, 1, TOK), I32),
            pltpu.VMEM(tiles, BF16),
            pltpu.VMEM(tiles, BF16),
            pltpu.VMEM(tiles, BF16),
            pltpu.VMEM(tiles, BF16),
            pltpu.VMEM(kv_tiles, BF16),
            pltpu.VMEM(kv_tiles, BF16),
            pltpu.VMEM(kv_tiles, BF16),
            pltpu.VMEM(kv_tiles, BF16),
            pltpu.VMEM((2, 1, TOK), I32),
            pltpu.VMEM((16 * PEERS, 4 * IMG), BF16),
            pltpu.VMEM((4 * IMG, 16 * PEERS), BF16),
            pltpu.VMEM((4 * TOK, 16 * PEERS), BF16),
            pltpu.VMEM((16 * PEERS, 4 * TOK), BF16),
            pltpu.VMEM((2 * TOK, 256), F32),
            pltpu.VMEM((TOK, 256), F32),
            pltpu.VMEM((TOK, 128), F32),
            pltpu.VMEM((KEY_VALUE_HEADS, KEYS, 256), BF16),
            pltpu.VMEM((GROUP * TOK, 128), BF16),
            pltpu.VMEM((KEYS, GROUP * TOK), BF16),
            pltpu.VMEM((KEYS, GROUP * TOK), BF16),
            pltpu.VMEM(halo, BF16),
            pltpu.VMEM(halo, F32),
            pltpu.VMEM(halo, F32),
            pltpu.VMEM(halo, BF16),
            pltpu.VMEM(halo, BF16),
            pltpu.VMEM(halo, BF16),
            pltpu.VMEM(halo, BF16),
            dma((7,)),
            dma, dma,
            dma((PARTS,)), dma((PARTS,)), dma((PARTS,)), dma((PARTS,)),
            dma((2,)), dma((2,)),
            dma((4,)), dma((4,)), dma((4,)), dma((4,)),
            dma((4,)), dma((4,)), dma((4,)), dma((4,)),
        ],
        compiler_params=pltpu.CompilerParams(
            collective_id=0, has_side_effects=True, vmem_limit_bytes=58 << 20
        ),
        cost_estimate=pl.CostEstimate(
            flops=4 << 30, bytes_accessed=5 << 20, transcendentals=2 << 20
        ),
    )(
        text_qkv[0, 0], segments[0], image_qkv[0, 0, 0], patch_counts[0, 0],
        image_dest[0, 0], image_offset[0, 0], output_cotangent[0, 0],
    )
    text_grad, image_grad = pl.pallas_call(
        write_out,
        name="write_out",
        out_shape=(
            jax.ShapeDtypeStruct((TOK, COLS), BF16),
            jax.ShapeDtypeStruct((IMG, COLS), BF16),
        ),
        in_specs=[vmem, vmem],
        out_specs=(hbm, hbm),
        scratch_shapes=[dma((2,))],
        compiler_params=pltpu.CompilerParams(vmem_limit_bytes=4 << 20),
    )(text_grad, image_grad)
    return text_grad[None, None], image_grad[None, None, None]


def solution(mesh):
    rows = P("enc", "llm", "sp", None)
    deep = P("enc", "llm", "sp", None, None)
    return jax.shard_map(
        body, mesh=mesh,
        in_specs=(rows, P("enc", "llm", "sp"), deep, rows, rows, rows, rows),
        out_specs=(rows, deep), check_vma=False,
    )
```

```python
import jax
import jax.numpy as jnp
from jax import lax
from jax.experimental import pallas as pl
from jax.experimental.pallas import tpu as pltpu
from jax.sharding import PartitionSpec as P

QUERY_HEADS = 32
KEY_VALUE_HEADS = 4
HEAD_SIZE = 128
TOK = 128
IMG = 64
PATCHES = 32
N_ENC = 8
N_LLM = 4
N_SP = 16
PEERS = N_ENC * N_LLM
SLOTS = 4
COLS = (QUERY_HEADS + 2 * KEY_VALUE_HEADS) * HEAD_SIZE
GROUP = QUERY_HEADS // KEY_VALUE_HEADS
KEYS = 3 * TOK
PARTS = 6
PART = 1024
SCALE = HEAD_SIZE ** (-0.5)
EXP2_SCALE = SCALE * 1.4426950408889634
HIDDEN = -1e30

MESH = pl.DeviceIdType.MESH
F32 = jnp.float32
BF16 = jnp.bfloat16
I32 = jnp.int32


def iota(shape, dim):
    return lax.broadcasted_iota(I32, shape, dim)


def dot(a, b):
    return jnp.dot(a, b, preferred_element_type=F32)


def dot_t(a, b):
    return lax.dot_general(a, b, (((1,), (1,)), ((), ())), preferred_element_type=F32)


def as_column(row, size):
    eye = iota((size, size), 0) == iota((size, size), 1)
    return jnp.sum(jnp.where(eye, row, 0.0), axis=1, keepdims=True)


def one_hot(condition):
    return jnp.where(condition, 1.0, 0.0).astype(BF16)


def kernel(
    text_hbm, seg_hbm, img_hbm, count_hbm, dest_hbm, offset_hbm, cot_hbm,
    text_grad, image_grad,
    text, seg, img, count, dest, offset, cot,
    mark_out, mark_in, row_out, row_in, grad_out, grad_in,
    kv_rows_out, kv_rows_in, kv_grads_out, kv_grads_in, seg_in,
    pack, unpack, place, collect, bias, causal, image_mask,
    kv, queries, probs_t, ds_t, far, near, own, far_in, pass_out, pass_in, kv_grad,
    load_sem, mark_send, mark_recv, row_send, row_recv, grad_send, grad_recv,
    seg_send, seg_recv, kv_send, kv_recv, relay_send, relay_recv,
    far_send, far_recv, pass_send, pass_recv,
):
    e, l, s = lax.axis_index("enc"), lax.axis_index("llm"), lax.axis_index("sp")
    me = e * N_LLM + l
    up, up2, down, down2 = (lax.rem(s + d, N_SP) for d in (1, 2, N_SP - 1, N_SP - 2))

    loads = [
        pltpu.make_async_copy(src, dst, load_sem.at[i])
        for i, (src, dst) in enumerate(
            (
                (dest_hbm, dest), (offset_hbm, offset), (count_hbm, count), (seg_hbm, seg),
                (img_hbm, img), (text_hbm, text), (cot_hbm, cot),
            )
        )
    ]
    for load in loads:
        load.start()

    barrier = pltpu.get_barrier_semaphore()

    def peer(i):
        p = lax.rem(me + i, PEERS)
        return p, (p // N_LLM, lax.rem(p, N_LLM), s)

    def greet(i, carry):
        pl.semaphore_signal(barrier, inc=1, device_id=peer(i)[1], device_id_type=MESH)
        return carry

    lax.fori_loop(1, PEERS, greet, 0)
    for z in (down, down2, up):
        pl.semaphore_signal(barrier, inc=1, device_id=(e, l, z), device_id_type=MESH)

    for load in loads[:3]:
        load.wait()
    row_id = iota((1, IMG), 1)
    counts = jnp.where(row_id < PATCHES, count[:, 0:1], count[:, 1:2])
    live_row = lax.rem(row_id, PATCHES) < counts
    dest_row = jnp.where(live_row, dest[...], -1).astype(F32)
    dest_col = as_column(dest_row, IMG)
    offset_col = as_column(offset[...].astype(F32), IMG)
    same = (dest_col == dest_row) & (dest_row >= 0.0)
    lower = iota((IMG, IMG), 1) < iota((IMG, IMG), 0)
    higher = iota((IMG, IMG), 0) < iota((IMG, IMG), 1)
    rank_col = jnp.sum(jnp.where(same & lower, 1.0, 0.0), axis=1, keepdims=True)
    rank_row = jnp.sum(jnp.where(same & higher, 1.0, 0.0), axis=0, keepdims=True)
    slot_row = jnp.where(dest_row >= 0.0, dest_row * SLOTS + rank_row, -1.0)
    slot_col = jnp.where(dest_col >= 0.0, dest_col * SLOTS + rank_col, -1.0)
    repeat = one_hot(lax.rem(iota((IMG, 4 * IMG), 1), IMG) == iota((IMG, 4 * IMG), 0))
    slots_row = dot(jnp.broadcast_to(slot_row, (8, IMG)).astype(BF16), repeat)[0:1, :]
    codes_row = slots_row.astype(I32) * 4 + iota((1, 4 * IMG), 1) // IMG
    pack[...] = one_hot(iota((16 * PEERS, 4 * IMG), 0) == codes_row)
    to_whom = one_hot(iota((PEERS, IMG), 0).astype(F32) == dest_row)
    lane = iota((IMG, TOK), 1)
    marks_mine = jnp.where(
        lane.astype(F32) == (me * SLOTS).astype(F32) + rank_col, offset_col + 1.0, 0.0
    ).astype(BF16)
    marks = dot(to_whom, marks_mine).astype(I32)
    for d in range(PEERS):
        mark_out[d] = marks[d : d + 1, :]
    mark_in[pl.ds(me, 1)] = mark_out[pl.ds(me, 1)]

    def four_tall(read, tiles):
        return jnp.concatenate(
            [jnp.concatenate([read(t, b) for b in range(4)], axis=0) for t in tiles], axis=1
        )

    def q_columns(g, t, b):
        return pl.ds(pl.multiple_of(g * PART + t * 512 + b * 128, 128), 128)

    def kv_columns(g, t):
        return slice(4096 + t * 512 + g * 128, 4096 + t * 512 + g * 128 + 128)

    def pack_queries(g):
        packed = dot(pack[...], four_tall(lambda t, b: img[:, q_columns(g, t, b)], (0, 1)))
        packed = packed.astype(BF16)
        for t in range(2):
            row_out[g, :, t] = packed[:, t * 128 : (t + 1) * 128].reshape(PEERS, 16, 128)
        row_in[g, pl.ds(me, 1)] = row_out[g, pl.ds(me, 1)]

    def pack_kv():
        packed = dot(
            pack[...],
            four_tall(lambda t, b: img[:, kv_columns(2 * t + b // 2, b % 2)], (0, 1)),
        ).astype(BF16)
        for t in range(2):
            kv_rows_out[t] = packed[:, t * 128 : (t + 1) * 128].reshape(PEERS, 16, 128)
            kv_rows_in[t, pl.ds(me, 1)] = kv_rows_out[t, pl.ds(me, 1)]

    def scatter(source, target, send_sem, recv_sem):
        def copy_of(i):
            p, device = peer(i)
            return pltpu.make_async_remote_copy(
                src_ref=source.at[p], dst_ref=target.at[me], send_sem=send_sem,
                recv_sem=recv_sem, device_id=device, device_id_type=MESH,
            )

        def two(n, carry):
            copy_of(PEERS // 2 - n).start()
            copy_of(PEERS // 2 + n).start()
            return carry

        copy_of(PEERS // 2).start()
        lax.fori_loop(1, PEERS // 2, two, 0)

    def whole(source, target, send_sem, recv_sem):
        return pltpu.make_async_remote_copy(
            src_ref=source.at[0 : PEERS - 1], dst_ref=target.at[0 : PEERS - 1],
            send_sem=send_sem, recv_sem=recv_sem, device_id=(e, l, up), device_id_type=MESH,
        )

    def rows_of(g):
        return row_out.at[g], row_in.at[g], row_send.at[g], row_recv.at[g]

    def kv_rows_of(t):
        return kv_rows_out.at[t], kv_rows_in.at[t], row_send.at[4 + t], row_recv.at[4 + t]

    def grads_of(g):
        return grad_out.at[g], grad_in.at[g], grad_send.at[g], grad_recv.at[g]

    def kv_grads_of(t):
        return kv_grads_out.at[t], kv_grads_in.at[t], grad_send.at[4 + t], grad_recv.at[4 + t]

    marks_of = (mark_out, mark_in, mark_send, mark_recv)

    loads[4].wait()
    pack_kv()
    loads[3].wait()
    pl.semaphore_wait(barrier, PEERS + 2)
    scatter(*marks_of)
    scatter(*kv_rows_of(0))
    scatter(*kv_rows_of(1))
    seg_copies = [
        pltpu.make_async_remote_copy(
            src_ref=seg, dst_ref=seg_in.at[i], send_sem=seg_send.at[i], recv_sem=seg_recv.at[i],
            device_id=(e, l, z), device_id_type=MESH,
        )
        for i, z in enumerate((up, up2))
    ]
    for copy in seg_copies:
        copy.start()

    def send_queries(g, carry):
        pack_queries(g)
        scatter(*rows_of(g))
        return carry

    lax.fori_loop(0, KEY_VALUE_HEADS, send_queries, 0)

    slots_col = jnp.concatenate([slot_col] * 4, axis=0)
    codes_col = slots_col.astype(I32) * 4 + iota((4 * IMG, 1), 0) // IMG
    unpack[...] = one_hot(codes_col == iota((4 * IMG, 16 * PEERS), 1))

    for copy in seg_copies:
        copy.wait_recv()
    seg_row = seg[...].astype(F32)
    seg_near = jnp.where(s >= 1, as_column(seg_in[0].astype(F32), TOK), -1.0)
    seg_far = jnp.where(s >= 2, as_column(seg_in[1].astype(F32), TOK), -1.0)
    seg_own = as_column(seg_row, TOK)
    earlier = iota((TOK, TOK), 0) <= iota((TOK, TOK), 1)
    near_bias = jnp.where(seg_near == seg_row, 0.0, HIDDEN)
    rest_bias = jnp.where(jnp.where(earlier, seg_own, seg_far) == seg_row, 0.0, HIDDEN)
    for h in range(2):
        half = slice(h * 128, (h + 1) * 128)
        bias[0:TOK, half] = rest_bias
        bias[TOK : 2 * TOK, half] = near_bias
        causal[:, half] = jnp.where(earlier, 1.0, 0.0)

    whole(*marks_of).wait_recv()
    marks_row = jnp.sum(mark_in[...], axis=0).astype(F32)
    spread = one_hot(iota((TOK, 16 * PEERS), 0) == iota((TOK, 16 * PEERS), 1) // 4)
    spread_row = dot(jnp.broadcast_to(marks_row, (8, TOK)).astype(BF16), spread)[0:1, :]
    codes_row = spread_row.astype(I32) + lax.rem(iota((1, 16 * PEERS), 1), 4) * 256
    tall = iota((4 * TOK, 1), 0)
    codes_col = lax.rem(tall, TOK) + 1 + tall // TOK * 256
    place[...] = one_hot(codes_col == codes_row)
    taken = jnp.sum(
        jnp.where((iota((TOK, TOK), 0) + 1).astype(F32) == marks_row, 1.0, 0.0),
        axis=1, keepdims=True,
    )
    image_mask[...] = jnp.broadcast_to(taken, (TOK, TOK))
    loads[5].wait()

    def mixed(landed, text_rows):
        return jnp.where(image_mask[...] > 0.0, landed, text_rows.astype(F32)).astype(BF16)

    def masked(rows):
        return jnp.where(image_mask[...] > 0.0, 0.0, rows).astype(BF16)

    def next_copy(g):
        return pltpu.make_async_remote_copy(
            src_ref=kv.at[g, 2 * TOK : 3 * TOK], dst_ref=kv.at[g, TOK : 2 * TOK],
            send_sem=kv_send.at[g], recv_sem=kv_recv.at[g],
            device_id=(e, l, up), device_id_type=MESH,
        )

    def relay_copy(g):
        return pltpu.make_async_remote_copy(
            src_ref=kv.at[g, TOK : 2 * TOK], dst_ref=kv.at[g, 0:TOK],
            send_sem=relay_send.at[g], recv_sem=relay_recv.at[g],
            device_id=(e, l, up), device_id_type=MESH,
        )

    def far_copy(g):
        return pltpu.make_async_remote_copy(
            src_ref=far.at[g], dst_ref=far_in.at[g],
            send_sem=far_send.at[g], recv_sem=far_recv.at[g],
            device_id=(e, l, down), device_id_type=MESH,
        )

    def pass_copy(g):
        return pltpu.make_async_remote_copy(
            src_ref=pass_out.at[g], dst_ref=pass_in.at[g],
            send_sem=pass_send.at[g], recv_sem=pass_recv.at[g],
            device_id=(e, l, down), device_id_type=MESH,
        )

    def relay(g):
        next_copy(g).wait_recv()
        relay_copy(g).start()

    def place_kv(t):
        whole(*kv_rows_of(t)).wait_recv()
        landed = dot(place[...], kv_rows_in[t].reshape(16 * PEERS, 128))
        for b in range(4):
            g, half = 2 * t + b // 2, b % 2
            kv[g, 2 * TOK : 3 * TOK, half * 128 : (half + 1) * 128] = mixed(
                landed[b * 128 : (b + 1) * 128], text[:, kv_columns(g, half)]
            )

    place_kv(0)
    next_copy(0).start()
    next_copy(1).start()
    place_kv(1)

    tall = iota((16 * PEERS, TOK), 0)
    spread_col = jnp.sum(
        jnp.where(iota((16 * PEERS, TOK), 1) == tall // 4, marks_row, 0.0),
        axis=1, keepdims=True,
    )
    codes_col = spread_col.astype(I32) + lax.rem(iota((16 * PEERS, 1), 0), 4) * 256
    wide = iota((1, 4 * TOK), 1)
    collect[...] = one_hot(codes_col == lax.rem(wide, TOK) + 1 + wide // TOK * 256)

    relay(0)
    next_copy(2).start()
    relay(1)
    next_copy(3).start()

    def chain(g):
        far_copy(g).wait_recv()
        pass_out[g] = (near[g] + far_in[g].astype(F32)).astype(BF16)
        pass_copy(g).start()

    def finish(g):
        pass_copy(g).wait_recv()
        kv_grad[g] = (own[g] + pass_in[g].astype(F32)).astype(BF16)

    loads[6].wait()

    def back(g, carry):
        grads_t = dot(kv[g, :, 0:128].T, ds_t[g]).astype(BF16)
        grads = [grads_t[:, h * 128 : (h + 1) * 128].T for h in range(GROUP)]
        gathered = dot(collect[...], four_tall(lambda t, b: grads[t * 4 + b], (0, 1)))
        gathered = gathered.astype(BF16)
        for t in range(2):
            grad_out[g, :, t] = gathered[:, t * 128 : (t + 1) * 128].reshape(PEERS, 16, 128)
        grad_in[g, pl.ds(me, 1)] = grad_out[g, pl.ds(me, 1)]
        scatter(*grads_of(g))
        for t in range(2):
            for b in range(4):
                text_grad[:, q_columns(g, t, b)] = masked(grads[t * 4 + b].astype(F32))
        return carry

    def group(g, carry):
        whole(*rows_of(g)).wait_recv()
        arrived = jnp.concatenate(
            [row_in[g, :, t].reshape(16 * PEERS, 128) for t in range(2)], axis=1
        )
        landed = dot(place[...], arrived)
        for t in range(2):
            for b in range(4):
                h = t * 4 + b
                queries[h * 128 : (h + 1) * 128, :] = mixed(
                    landed[b * 128 : (b + 1) * 128, t * 128 : (t + 1) * 128],
                    text[:, q_columns(g, t, b)],
                )

        relay_copy(g).wait_recv()
        keys = kv[g, :, 0:128]
        values = kv[g, :, 128:256]
        cots = [
            cot[:, pl.ds(pl.multiple_of(g * PART + h * 128, 128), 128)] for h in range(GROUP)
        ]
        is_own = causal[...] > 0.0
        own_part = causal[...].astype(BF16)
        far_part = (1.0 - causal[...]).astype(BF16)

        def two_blocks(products):
            rest = jnp.where(is_own, products[2 * TOK :], products[0:TOK])
            return jnp.concatenate([rest, products[TOK : 2 * TOK]], axis=0)

        for pair in range(GROUP // 2):
            both = slice(pair * 256, (pair + 1) * 256)
            d_out = jnp.concatenate(cots[2 * pair : 2 * pair + 2], axis=0)
            logits = two_blocks(dot_t(keys, queries[both, :])) + bias[...]
            grad_probs = two_blocks(dot_t(values, d_out))
            top = jnp.max(logits, axis=0, keepdims=True)
            raised = jnp.exp2((logits - top) * EXP2_SCALE)
            inverse = 1.0 / jnp.sum(raised, axis=0, keepdims=True)
            delta = jnp.sum(raised * grad_probs, axis=0, keepdims=True) * inverse
            probs = (raised * inverse).astype(BF16)
            ds = (raised * ((grad_probs - delta) * (inverse * SCALE))).astype(BF16)
            for target, value in ((probs_t, probs), (ds_t.at[g], ds)):
                target[0:TOK, both] = value[0:TOK] * far_part
                target[TOK : 2 * TOK, both] = value[TOK : 2 * TOK]
                target[2 * TOK : 3 * TOK, both] = value[0:TOK] * own_part
        key_grad = dot(ds_t[g], queries[...])
        value_grad = dot(probs_t[...], jnp.concatenate(cots, axis=0))
        for t, grad in enumerate((key_grad, value_grad)):
            half = slice(t * 128, (t + 1) * 128)
            far[g, :, half] = grad[0:TOK].astype(BF16)
            near[g, :, half] = grad[TOK : 2 * TOK]
            own[g, :, half] = grad[2 * TOK : 3 * TOK]
        far_copy(g).start()

        @pl.when(g < 2)
        def _():
            relay(g + 2)

        @pl.when(g >= 1)
        def _():
            chain(g - 1)

        @pl.when(g < 2)
        def _():
            back(g, 0)

        @pl.when(g >= 2)
        def _():
            finish(g - 2)

        return carry

    lax.fori_loop(0, KEY_VALUE_HEADS, group, 0)

    def return_kv(t):
        rows = four_tall(
            lambda _, b: kv_grad[2 * t + b // 2, :, b % 2 * 128 : (b % 2 + 1) * 128], (0,)
        )
        kv_grads_out[t] = dot(collect[...], rows).astype(BF16).reshape(PEERS, 16, 128)
        kv_grads_in[t, pl.ds(me, 1)] = kv_grads_out[t, pl.ds(me, 1)]
        scatter(*kv_grads_of(t))

    def take_back(g, carry):
        whole(*grads_of(g)).wait_recv()
        returned = jnp.concatenate(
            [grad_in[g, :, t].reshape(16 * PEERS, 128) for t in range(2)], axis=1
        )
        back = dot(unpack[...], returned).astype(BF16)
        for t in range(2):
            for b in range(4):
                image_grad[:, q_columns(g, t, b)] = back[
                    b * IMG : (b + 1) * IMG, t * 128 : (t + 1) * 128
                ]
        return carry

    lax.fori_loop(2, KEY_VALUE_HEADS, back, 0)
    chain(3)
    return_kv(0)
    finish(2)
    finish(3)
    return_kv(1)
    for g in range(KEY_VALUE_HEADS):
        for t in range(2):
            text_grad[:, kv_columns(g, t)] = masked(
                kv_grad[g, :, t * 128 : (t + 1) * 128].astype(F32)
            )
    lax.fori_loop(0, KEY_VALUE_HEADS, take_back, 0)

    whole(*marks_of).wait_send()
    for copy in seg_copies:
        copy.wait_send()

    def drain(g, carry):
        whole(*rows_of(g)).wait_send()
        whole(*grads_of(g)).wait_send()
        for copy in (next_copy, relay_copy, far_copy, pass_copy):
            copy(g).wait_send()
        return carry

    lax.fori_loop(0, KEY_VALUE_HEADS, drain, 0)
    for t in range(2):
        whole(*kv_rows_of(t)).wait_send()
        whole(*kv_grads_of(t)).wait()
        back = dot(unpack[...], kv_grads_in[t].reshape(16 * PEERS, 128)).astype(BF16)
        for b in range(4):
            image_grad[:, kv_columns(2 * t + b // 2, b % 2)] = back[b * IMG : (b + 1) * IMG]


def write_out(text_grad, image_grad, text_out, image_out, sem):
    copies = [
        pltpu.make_async_copy(text_grad, text_out, sem.at[0]),
        pltpu.make_async_copy(image_grad, image_out, sem.at[1]),
    ]
    for copy in copies:
        copy.start()
    for copy in copies:
        copy.wait()


def body(text_qkv, segments, image_qkv, patch_counts, image_dest, image_offset, output_cotangent):
    hbm = pl.BlockSpec(memory_space=pl.ANY)
    dma = pltpu.SemaphoreType.DMA
    q_cols = QUERY_HEADS * HEAD_SIZE
    tiles = (KEY_VALUE_HEADS, PEERS, 2, 16, 128)
    kv_tiles = (2, PEERS, 16, 128)
    vmem = pl.BlockSpec(memory_space=pltpu.VMEM)
    halo = (KEY_VALUE_HEADS, TOK, 256)
    text_grad, image_grad = pl.pallas_call(
        kernel,
        name="slab",
        out_shape=(pltpu.VMEM((TOK, COLS), BF16), pltpu.VMEM((IMG, COLS), BF16)),
        in_specs=[pl.BlockSpec(memory_space=pltpu.HBM)] * 7,
        out_specs=(vmem, vmem),
        scratch_shapes=[
            pltpu.VMEM((TOK, COLS), BF16),
            pltpu.VMEM((1, TOK), I32),
            pltpu.VMEM((IMG, COLS), BF16),
            pltpu.VMEM((1, 2), I32),
            pltpu.VMEM((1, IMG), I32),
            pltpu.VMEM((1, IMG), I32),
            pltpu.VMEM((TOK, q_cols), BF16),
            pltpu.VMEM((PEERS, 1, TOK), I32),
            pltpu.VMEM((PEERS, 1, TOK), I32),
            pltpu.VMEM(tiles, BF16),
            pltpu.VMEM(tiles, BF16),
            pltpu.VMEM(tiles, BF16),
            pltpu.VMEM(tiles, BF16),
            pltpu.VMEM(kv_tiles, BF16),
            pltpu.VMEM(kv_tiles, BF16),
            pltpu.VMEM(kv_tiles, BF16),
            pltpu.VMEM(kv_tiles, BF16),
            pltpu.VMEM((2, 1, TOK), I32),
            pltpu.VMEM((16 * PEERS, 4 * IMG), BF16),
            pltpu.VMEM((4 * IMG, 16 * PEERS), BF16),
            pltpu.VMEM((4 * TOK, 16 * PEERS), BF16),
            pltpu.VMEM((16 * PEERS, 4 * TOK), BF16),
            pltpu.VMEM((2 * TOK, 256), F32),
            pltpu.VMEM((TOK, 256), F32),
            pltpu.VMEM((TOK, 128), F32),
            pltpu.VMEM((KEY_VALUE_HEADS, KEYS, 256), BF16),
            pltpu.VMEM((GROUP * TOK, 128), BF16),
            pltpu.VMEM((KEYS, GROUP * TOK), BF16),
            pltpu.VMEM((KEY_VALUE_HEADS, KEYS, GROUP * TOK), BF16),
            pltpu.VMEM(halo, BF16),
            pltpu.VMEM(halo, F32),
            pltpu.VMEM(halo, F32),
            pltpu.VMEM(halo, BF16),
            pltpu.VMEM(halo, BF16),
            pltpu.VMEM(halo, BF16),
            pltpu.VMEM(halo, BF16),
            dma((7,)),
            dma, dma,
            dma((PARTS,)), dma((PARTS,)), dma((PARTS,)), dma((PARTS,)),
            dma((2,)), dma((2,)),
            dma((4,)), dma((4,)), dma((4,)), dma((4,)),
            dma((4,)), dma((4,)), dma((4,)), dma((4,)),
        ],
        compiler_params=pltpu.CompilerParams(
            collective_id=0, has_side_effects=True, vmem_limit_bytes=58 << 20
        ),
        cost_estimate=pl.CostEstimate(
            flops=4 << 30, bytes_accessed=5 << 20, transcendentals=2 << 20
        ),
    )(
        text_qkv[0, 0], segments[0], image_qkv[0, 0, 0], patch_counts[0, 0],
        image_dest[0, 0], image_offset[0, 0], output_cotangent[0, 0],
    )
    text_grad, image_grad = pl.pallas_call(
        write_out,
        name="write_out",
        out_shape=(
            jax.ShapeDtypeStruct((TOK, COLS), BF16),
            jax.ShapeDtypeStruct((IMG, COLS), BF16),
        ),
        in_specs=[vmem, vmem],
        out_specs=(hbm, hbm),
        scratch_shapes=[dma((2,))],
        compiler_params=pltpu.CompilerParams(vmem_limit_bytes=4 << 20),
    )(text_grad, image_grad)
    return text_grad[None, None], image_grad[None, None, None]


def solution(mesh):
    rows = P("enc", "llm", "sp", None)
    deep = P("enc", "llm", "sp", None, None)
    return jax.shard_map(
        body, mesh=mesh,
        in_specs=(rows, P("enc", "llm", "sp"), deep, rows, rows, rows, rows),
        out_specs=(rows, deep), check_vma=False,
    )
```
